256 devices in a mesh: prow: 8 (over x, core), pcol: 32 (over z, y).
Axes of the slice: x: 4, y: 4, z: 8, core: 2. Of those that a mesh axis runs over, the one named last changes fastest.
Arguments:
- trailing: float32 [16384, 16384], P('prow', 'pcol'), may hold values from -8 to 8
- panel: float32 [16384, 128], P(('prow', 'pcol')), may hold values from -3 to 3, as said below
Outputs:
- updated: float32 [16384, 16384], P('prow', 'pcol')
- reflectors: float32 [16384, 128], P('prow')
- factor: float32 [128, 128], replicated
- band_block: float32 [128, 128], replicated
- first_factor: float32 [128, 128], replicated
The draws below stay inside these ranges and needn't reach their ends.
Inputs may be any that keep to these rules, and one draw needn't show every extreme that they name: `panel`: rows 0 to 127 are twice the identity plus entries between 0 and 0.25.
All inputs are finite; a program needn't handle non-finite values.
Results may differ from the reference program's by a relative error of at most 0.0003.
Values sent between devices are 32-bit elements; how exact they have to be, the bound alone decides.
No kernel may reach another device: no remote copies, remote signals or barrier semaphores. Data moves between devices by JAX's collectives and lax.ppermute only.
A program may use at most 64 MiB of HBM per device.

```python
import jax
import jax.numpy as jnp
from jax import lax

M = 16384
NB = 128


def draw_trailing(key, part):
    key = jax.random.fold_in(key, 11)
    key_one = jax.random.fold_in(key, 0)
    raw_values = jnp.clip(jax.random.normal(key_one, (M, M), jnp.float32), -5.0, 5.0)
    return jnp.clip((raw_values + raw_values.T) * 0.70710678, -8.0, 8.0)


def draw_panel(key, part):
    key = jax.random.fold_in(key, 23)
    key_one = jax.random.fold_in(key, 0)
    key_two = jax.random.fold_in(key, 1)
    key_four = jax.random.fold_in(key, 3)
    key_five = jax.random.fold_in(key, 4)
    key_six = jax.random.fold_in(key, 5)
    spread = 4.0 / M ** 0.5
    row_common = jax.random.uniform(key_four, (M,), jnp.float32, -1.0, 1.0)
    col_sizes = jax.random.uniform(key_five, (NB,), jnp.float32, 0.5, 1.5)
    col_signs = jnp.where(jax.random.uniform(key_six, (NB,), jnp.float32, -1.0, 1.0) < 0.0, -1.0, 1.0)
    common_part = 1.6 * row_common[:, None] * (col_sizes * col_signs)[None, :]
    noise_part = jax.random.uniform(key_two, (M, NB), jnp.float32, 0.0, 0.25)
    base_rows = jax.random.normal(key_one, (M, NB), jnp.float32) * spread
    base_rows = jnp.clip(base_rows + common_part, -3.0, 3.0)
    row_ids = lax.broadcasted_iota(jnp.int32, (M, NB), 0)
    col_ids = lax.broadcasted_iota(jnp.int32, (M, NB), 1)
    top_rows = jnp.where(row_ids == col_ids, 2.0, 0.0) + noise_part
    return jnp.where(row_ids < NB, top_rows, base_rows)


def setup_inputs(seed: int = 0) -> dict:
    key_list = jax.random.split(jax.random.key(seed), 3)
    trailing = draw_trailing(jax.random.fold_in(key_list[2], 71), 0)
    panel = draw_panel(jax.random.fold_in(key_list[2], 71), 0)
    return dict(trailing=trailing, panel=panel)


HIGHEST_PREC = lax.Precision.HIGHEST

def product(left, right):
    return jnp.dot(left, right, precision=HIGHEST_PREC)

def lu_plain(square):
    order = square.shape[0]
    positions = jnp.arange(order)

    def elimination(column_at, packed):
        pivot_value = packed[column_at, column_at]
        below_col = jnp.where(positions > column_at, packed[:, column_at] / pivot_value, 0.0)
        right_row = jnp.where(positions > column_at, packed[column_at, :], 0.0)
        packed = packed - below_col[:, None] * right_row[None, :]
        return packed.at[:, column_at].set(jnp.where(positions > column_at, below_col, packed[:, column_at]))
    packed = lax.fori_loop(0, order, elimination, square)
    unit_lower = jnp.tril(packed, -1) + jnp.eye(order, dtype=packed.dtype)
    return (unit_lower, jnp.triu(packed))

def reference(trailing, panel):
    solve = jax.scipy.linalg.solve_triangular
    chol_one = jnp.linalg.cholesky(product(panel.T, panel))
    ortho_one = solve(chol_one, panel.T, lower=True).T
    chol_two = jnp.linalg.cholesky(product(ortho_one.T, ortho_one))
    ortho = solve(chol_two, ortho_one.T, lower=True).T
    band_block = product(chol_one, chol_two).T
    unit_lower, upper_part = lu_plain(ortho[:NB] + jnp.eye(NB, dtype=ortho.dtype))
    below_rows = solve(upper_part.T, ortho[NB:].T, lower=True).T
    reflectors = jnp.concatenate([unit_lower, below_rows], 0)
    factor = solve(unit_lower, upper_part.T, lower=True, unit_diagonal=True).T
    wide = product(product(trailing, reflectors), factor)
    inner = product(reflectors.T, wide)
    change = wide - 0.5 * product(reflectors, product(factor.T, inner))
    updated = trailing - product(reflectors, change.T)
    updated = updated - product(change, reflectors.T)
    return (updated, reflectors, factor, band_block, chol_one.T)
```

```python
import functools

import jax
import jax.numpy as jnp
from jax import lax
from jax.experimental import pallas as pl
from jax.experimental.pallas import tpu as pltpu
from jax.sharding import PartitionSpec as P

HIGHEST = lax.Precision.HIGHEST
ROWS, ZS, YS = 8, 8, 4
NN = (((1,), (0,)), ((), ()))
NT = (((1,), (1,)), ((), ()))
TN = (((0,), (0,)), ((), ()))


def dot(left, right, dims=NN, precision=HIGHEST):
    return lax.dot_general(
        left, right, dims, precision=precision, preferred_element_type=jnp.float32
    )


def recip(x):
    r = pl.reciprocal(x, approx=True)
    r = r * (2.0 - x * r)
    return r * (2.0 - x * r)


def eliminate(mats):
    n = mats[0].shape[0]
    lane = lax.broadcasted_iota(jnp.int32, (8, n), 1)
    sub = lax.broadcasted_iota(jnp.int32, (8, n), 0)
    across = lambda x, k: jnp.broadcast_to(x[:, k : k + 1], (8, n))
    down = lambda x, s: jnp.broadcast_to(x[s : s + 1], (8, n))
    tiles = [[m[8 * t : 8 * t + 8] for t in range(n // 8)] for m in mats]
    for t in range(n // 8):
        base = 8 * t
        block = (lane >= base) & (lane < base + 8)
        for m in tiles:
            cols = [across(m[t], base + s) for s in range(8)]
            work = m[t]
            invs, rows, heads = [], [], []
            for s in range(8):
                here = lane == base + s
                below = sub > s
                inv = recip(down(cols[s], s))
                row = jnp.where(here, 1.0, down(work, s))
                mult = jnp.where(below, cols[s] * inv, 0.0)
                work = jnp.where(here & below, 0.0, work) - mult * row
                head = [down(cols[q], s) for q in range(s + 1, 8)]
                for q in range(s + 1, 8):
                    cols[q] = cols[q] - mult * head[q - s - 1]
                invs.append(inv)
                rows.append(jnp.where(block & (lane > base + s), 0.0, row))
                heads.append(head)
            m[t] = work
            for j in range(t + 1, n // 8):
                cols = [across(m[j], base + s) for s in range(8)]
                new = jnp.where(block, 0.0, m[j])
                for s in range(8):
                    mult = cols[s] * invs[s]
                    new = new - mult * rows[s]
                    for q in range(s + 1, 8):
                        cols[q] = cols[q] - mult * heads[s][q - s - 1]
                m[j] = new
    return [jnp.concatenate(m, 0) for m in tiles]


def positions(n):
    row = lax.broadcasted_iota(jnp.int32, (n, n), 0)
    col = lax.broadcasted_iota(jnp.int32, (n, n), 1)
    return row, col


def cholesky_pair(gram):
    (packed,) = eliminate([gram])
    row, col = positions(gram.shape[0])
    pivots = jnp.sum(jnp.where(row == col, packed, 0.0), 1, keepdims=True)
    scale = 1.0 / jnp.sqrt(pivots)
    upper = jnp.where(col >= row, packed, 0.0) * scale
    inverse = jnp.where(col < row, packed, jnp.where(col == row, 1.0, 0.0)) * scale
    return upper, inverse


def first_kernel(gram_ref, upper_ref, inverse_ref):
    upper_ref[...], inverse_ref[...] = cholesky_pair(gram_ref[...])


def second_kernel(gram_ref, upper_one_ref, inverse_one_ref, leading_ref, inverse_two_ref, band_ref, band_inverse_t_ref, square_ref):
    upper, inverse = cholesky_pair(gram_ref[...])
    row, col = positions(upper.shape[0])
    inverse_one = inverse_one_ref[...]
    inverse_two_ref[...] = inverse
    band_ref[...] = dot(upper, upper_one_ref[...])
    band_inverse_t_ref[...] = dot(inverse, inverse_one)
    top = dot(dot(leading_ref[...], inverse_one, NT), inverse, NT)
    square_ref[...] = top + jnp.where(row == col, 1.0, 0.0)


def third_kernel(square_ref, factor_ref, upper_inverse_t_ref, square_inverse_ref):
    square = square_ref[...]
    one, two = eliminate([square, square.T])
    row, col = positions(square.shape[0])
    unit = jnp.where(row == col, 1.0, 0.0)
    pivots = jnp.sum(jnp.where(row == col, two, 0.0), 1, keepdims=True)
    upper = jnp.where(col >= row, one, 0.0)
    lower_inverse = jnp.where(col < row, one, unit)
    upper_inverse_t = jnp.where(col < row, two, unit) / pivots
    factor_ref[...] = dot(upper, lower_inverse, NT)
    upper_inverse_t_ref[...] = upper_inverse_t
    square_inverse_ref[...] = dot(upper_inverse_t, lower_inverse, TN)


def small_call(body, outs, name, *args):
    square = jax.ShapeDtypeStruct(args[0].shape, jnp.float32)
    return pl.pallas_call(
        body,
        out_shape=[square] * outs,
        name=name,
        cost_estimate=pl.CostEstimate(flops=1 << 33, bytes_accessed=1 << 20, transcendentals=0),
        compiler_params=pltpu.CompilerParams(vmem_limit_bytes=32 << 20),
    )(*args)


def swap_row(x, mask):
    return lax.ppermute(x, "prow", [(r, r ^ mask) for r in range(ROWS)])


def swap_y(x, mask):
    return lax.ppermute(x, "pcol", [(c, c ^ mask) for c in range(ZS * YS)])


def swap_z(x, mask):
    return lax.ppermute(x, "pcol", [(c, c ^ (mask * YS)) for c in range(ZS * YS)])


def transpose_chips(x):
    pairs = []
    for r in range(ROWS):
        for z in range(ZS):
            for y in range(YS):
                pairs.append((r * ZS * YS + z * YS + y, z * ZS * YS + r * YS + y))
    return lax.ppermute(x, ("prow", "pcol"), pairs)


def gather(x, swap, count, own):
    arrived = [swap(x, mask) for mask in range(1, count)]
    whole = jnp.zeros((count,) + x.shape, x.dtype)
    for mask, block in enumerate([x] + arrived):
        whole = lax.dynamic_update_index_in_dim(whole, block, own ^ mask, 0)
    return whole


def sum_rows(x):
    x = x + swap_row(x, 1)
    one, two, three = (swap_row(x, 2 * mask) for mask in (1, 2, 3))
    return (x + one) + (two + three)


def sum_rows_large(x, row_index):
    chip, core = row_index // 2, row_index % 2
    half = x.shape[0] // 2
    piece = half // 4
    other = swap_row(lax.dynamic_slice_in_dim(x, (1 - core) * half, half, 0), 1)
    mine = lax.dynamic_slice_in_dim(x, core * half, half, 0) + other
    parts = [
        lax.dynamic_slice_in_dim(mine, (chip ^ mask) * piece, piece, 0) for mask in range(4)
    ]
    one, two, three = (swap_row(parts[mask], 2 * mask) for mask in (1, 2, 3))
    part = (parts[0] + one) + (two + three)
    mine = gather(part, lambda v, mask: swap_row(v, 2 * mask), 4, chip).reshape(half, -1)
    return gather(mine, swap_row, 2, core).reshape(2 * half, -1)


def from_first_row(x, row_index):
    pair = lax.ppermute(x, "prow", [(0, 1)])
    pair = jnp.where(row_index == 0, x, pair)
    arrived = [
        lax.ppermute(pair, "prow", [(0, 2 * chip), (1, 2 * chip + 1)]) for chip in (1, 2, 3)
    ]
    return jnp.where(row_index < 2, pair, arrived[0] + arrived[1] + arrived[2])


def on_device(trailing, panel):
    rows, cols = trailing.shape
    chunk, width = panel.shape
    row_index = lax.axis_index("prow")
    col_index = lax.axis_index("pcol")
    z, y = col_index // YS, col_index % YS

    edge_cols = from_first_row(trailing[:width].T, row_index)
    edge_rows = gather(transpose_chips(edge_cols), swap_y, YS, y).reshape(rows, width)

    along_z = gather(panel, swap_z, ZS, z)
    panel_rows = gather(along_z, swap_y, YS, y)
    panel_rows = panel_rows.transpose(1, 0, 2, 3).reshape(rows, width)
    panel_cols = transpose_chips(lax.dynamic_slice_in_dim(panel_rows, y * cols, cols, 0))

    gram_one = sum_rows(dot(panel_rows, panel_rows, TN))

    product = dot(trailing, panel_rows, TN)
    leading = jnp.where(row_index == 0, panel_rows[:width], 0.0)
    summed = sum_rows_large(jnp.concatenate([product, leading], 0), row_index)
    product_cols, leading = summed[:cols], summed[cols:]
    product_rows = gather(transpose_chips(product_cols), swap_y, YS, y).reshape(rows, width)

    upper_one, inverse_one = small_call(first_kernel, 2, "first", gram_one)
    ortho_rows = dot(panel_rows, inverse_one, NT)
    gram_two = sum_rows(dot(ortho_rows, ortho_rows, TN))
    inverse_two, band_block, band_inverse_t, square = small_call(
        second_kernel, 4, "second", gram_two, upper_one, inverse_one, leading
    )

    def unit_rows(start, count):
        place = start + lax.broadcasted_iota(jnp.int32, (count, width), 0)
        return jnp.where(place == lax.broadcasted_iota(jnp.int32, (count, width), 1), 1.0, 0.0)

    base_rows = dot(ortho_rows, inverse_two, NT) + unit_rows(row_index * rows, rows)
    image_rows = dot(product_rows, band_inverse_t, NT) + edge_rows
    weight = sum_rows(dot(base_rows, image_rows, TN))
    ortho_cols = dot(dot(panel_cols, inverse_one, NT), inverse_two, NT)
    base_cols = ortho_cols + unit_rows(col_index * cols, cols)
    image_cols = dot(product_cols, band_inverse_t, NT) + edge_cols

    factor, upper_inverse_t, square_inverse = small_call(third_kernel, 3, "third", square)
    reflectors = dot(base_rows, upper_inverse_t, NT)
    place = row_index * rows + lax.broadcasted_iota(jnp.int32, (rows, width), 0)
    lane = lax.broadcasted_iota(jnp.int32, (rows, width), 1)
    reflectors = jnp.where(place < lane, 0.0, jnp.where(place == lane, 1.0, reflectors))

    left_rows = dot(base_rows, square_inverse)
    left_cols = dot(base_cols, square_inverse)
    right_rows = image_rows - 0.5 * dot(left_rows, weight)
    right_cols = image_cols - 0.5 * dot(left_cols, weight)
    updated = trailing - dot(
        jnp.concatenate([left_rows, right_rows], 1),
        jnp.concatenate([right_cols, left_cols], 1),
        NT,
    )
    return (updated, reflectors, factor, band_block, upper_one)


def solution(mesh):
    placed = (P("prow", "pcol"), P(("prow", "pcol"), None))
    return jax.shard_map(
        on_device,
        mesh=mesh,
        in_specs=placed,
        out_specs=(P("prow", "pcol"), P("prow", None), P(), P(), P()),
        check_vma=False,
    )
```

```python
import functools

import jax
import jax.numpy as jnp
from jax import lax
from jax.experimental import pallas as pl
from jax.experimental.pallas import tpu as pltpu
from jax.sharding import PartitionSpec as P

HIGHEST = lax.Precision.HIGHEST
ROWS, ZS, YS = 8, 8, 4
NN = (((1,), (0,)), ((), ()))
NT = (((1,), (1,)), ((), ()))
TN = (((0,), (0,)), ((), ()))


def dot(left, right, dims=NN, precision=HIGHEST):
    return lax.dot_general(
        left, right, dims, precision=precision, preferred_element_type=jnp.float32
    )


def recip(x):
    r = pl.reciprocal(x, approx=True)
    r = r * (2.0 - x * r)
    return r * (2.0 - x * r)


def eliminate(mats):
    n = mats[0].shape[0]
    lane = lax.broadcasted_iota(jnp.int32, (8, n), 1)
    sub = lax.broadcasted_iota(jnp.int32, (8, n), 0)
    across = lambda x, k: jnp.broadcast_to(x[:, k : k + 1], (8, n))
    down = lambda x, s: jnp.broadcast_to(x[s : s + 1], (8, n))
    tiles = [[m[8 * t : 8 * t + 8] for t in range(n // 8)] for m in mats]
    for t in range(n // 8):
        base = 8 * t
        block = (lane >= base) & (lane < base + 8)
        for m in tiles:
            cols = [across(m[t], base + s) for s in range(8)]
            work = m[t]
            invs, rows, heads = [], [], []
            for s in range(8):
                here = lane == base + s
                below = sub > s
                inv = recip(down(cols[s], s))
                row = jnp.where(here, 1.0, down(work, s))
                mult = jnp.where(below, cols[s] * inv, 0.0)
                work = jnp.where(here & below, 0.0, work) - mult * row
                head = [down(cols[q], s) for q in range(s + 1, 8)]
                for q in range(s + 1, 8):
                    cols[q] = cols[q] - mult * head[q - s - 1]
                invs.append(inv)
                rows.append(jnp.where(block & (lane > base + s), 0.0, row))
                heads.append(head)
            m[t] = work
            for j in range(t + 1, n // 8):
                cols = [across(m[j], base + s) for s in range(8)]
                new = jnp.where(block, 0.0, m[j])
                for s in range(8):
                    mult = cols[s] * invs[s]
                    new = new - mult * rows[s]
                    for q in range(s + 1, 8):
                        cols[q] = cols[q] - mult * heads[s][q - s - 1]
                m[j] = new
    return [jnp.concatenate(m, 0) for m in tiles]


def positions(n):
    row = lax.broadcasted_iota(jnp.int32, (n, n), 0)
    col = lax.broadcasted_iota(jnp.int32, (n, n), 1)
    return row, col


def cholesky_pair(gram):
    (packed,) = eliminate([gram])
    row, col = positions(gram.shape[0])
    pivots = jnp.sum(jnp.where(row == col, packed, 0.0), 1, keepdims=True)
    scale = 1.0 / jnp.sqrt(pivots)
    upper = jnp.where(col >= row, packed, 0.0) * scale
    inverse = jnp.where(col < row, packed, jnp.where(col == row, 1.0, 0.0)) * scale
    return upper, inverse


def first_kernel(gram_ref, upper_ref, inverse_ref):
    upper_ref[...], inverse_ref[...] = cholesky_pair(gram_ref[...])


def second_kernel(gram_ref, upper_one_ref, inverse_one_ref, leading_ref, inverse_two_ref, band_ref, band_inverse_t_ref, square_ref):
    upper, inverse = cholesky_pair(gram_ref[...])
    row, col = positions(upper.shape[0])
    inverse_one = inverse_one_ref[...]
    inverse_two_ref[...] = inverse
    band_ref[...] = dot(upper, upper_one_ref[...])
    band_inverse_t_ref[...] = dot(inverse, inverse_one)
    top = dot(dot(leading_ref[...], inverse_one, NT), inverse, NT)
    square_ref[...] = top + jnp.where(row == col, 1.0, 0.0)


def third_kernel(square_ref, factor_ref, upper_inverse_t_ref, square_inverse_ref):
    square = square_ref[...]
    one, two = eliminate([square, square.T])
    row, col = positions(square.shape[0])
    unit = jnp.where(row == col, 1.0, 0.0)
    pivots = jnp.sum(jnp.where(row == col, two, 0.0), 1, keepdims=True)
    upper = jnp.where(col >= row, one, 0.0)
    lower_inverse = jnp.where(col < row, one, unit)
    upper_inverse_t = jnp.where(col < row, two, unit) / pivots
    factor_ref[...] = dot(upper, lower_inverse, NT)
    upper_inverse_t_ref[...] = upper_inverse_t
    square_inverse_ref[...] = dot(upper_inverse_t, lower_inverse, TN)


def small_call(body, outs, name, *args):
    square = jax.ShapeDtypeStruct(args[0].shape, jnp.float32)
    return pl.pallas_call(
        body,
        out_shape=[square] * outs,
        name=name,
        cost_estimate=pl.CostEstimate(flops=1 << 33, bytes_accessed=1 << 20, transcendentals=0),
        compiler_params=pltpu.CompilerParams(vmem_limit_bytes=32 << 20),
    )(*args)


def swap_row(x, mask):
    return lax.ppermute(x, "prow", [(r, r ^ mask) for r in range(ROWS)])


def swap_y(x, mask):
    return lax.ppermute(x, "pcol", [(c, c ^ mask) for c in range(ZS * YS)])


def swap_z(x, mask):
    return lax.ppermute(x, "pcol", [(c, c ^ (mask * YS)) for c in range(ZS * YS)])


def transpose_chips(x):
    pairs = []
    for r in range(ROWS):
        for z in range(ZS):
            for y in range(YS):
                pairs.append((r * ZS * YS + z * YS + y, z * ZS * YS + r * YS + y))
    return lax.ppermute(x, ("prow", "pcol"), pairs)


def sum_rows(x):
    x = x + swap_row(x, 1)
    one, two, three = (swap_row(x, 2 * mask) for mask in (1, 2, 3))
    return (x + one) + (two + three)


def hold(*arrays):
    return lax.optimization_barrier(arrays)


def block_call(body, outs, name, cost, args, **more):
    return pl.pallas_call(
        body,
        out_shape=[jax.ShapeDtypeStruct(shape, jnp.float32) for shape in outs],
        name=name,
        cost_estimate=pl.CostEstimate(flops=cost, bytes_accessed=1 << 20, transcendentals=0),
        compiler_params=pltpu.CompilerParams(vmem_limit_bytes=40 << 20),
        **more,
    )(*args)


def whole(count):
    return [pl.BlockSpec(memory_space=pltpu.VMEM)] * count


def assemble_kernel(place_ref, *refs):
    stacks, out_ref = refs[:-1], refs[-1]
    chunk = stacks[0].shape[0] // ZS
    z, y = place_ref[1] // YS, place_ref[1] % YS
    for far_y, stack in enumerate(stacks):
        for far_z in range(ZS):
            at = ((z ^ far_z) * YS + (y ^ far_y)) * chunk
            out_ref[pl.ds(pl.multiple_of(at, chunk), chunk), :] = stack[
                chunk * far_z : chunk * (far_z + 1), :
            ]


def unit_rows(start, count, width):
    place = start + lax.broadcasted_iota(jnp.int32, (count, width), 0)
    return jnp.where(place == lax.broadcasted_iota(jnp.int32, (count, width), 1), 1.0, 0.0)


def image_kernel(place_ref, *refs):
    products, edges = refs[:YS], refs[YS : 2 * YS]
    ortho_ref, panel_ref, product_ref, edge_ref, inverse_one_ref, inverse_two_ref, band_inverse_t_ref = refs[2 * YS : 2 * YS + 7]
    base_ref, image_ref, weight_ref, base_cols_ref, image_cols_ref = refs[2 * YS + 7 :]
    cols, width = products[0].shape
    y = place_ref[1] % YS
    inverse_two = inverse_two_ref[...]
    band_inverse_t = band_inverse_t_ref[...]
    weight = jnp.zeros((width, width), jnp.float32)
    for far in range(YS):
        at = pl.multiple_of((y ^ far) * cols, cols)
        span = pl.ds(at, cols)
        start = place_ref[0] * (YS * cols) + at
        base = dot(ortho_ref[span, :], inverse_two, NT) + unit_rows(start, cols, width)
        image = dot(products[far][...], band_inverse_t, NT) + edges[far][...]
        base_ref[span, :] = base
        image_ref[span, :] = image
        weight = weight + dot(base, image, TN)
    weight_ref[...] = weight
    ortho_cols = dot(dot(panel_ref[...], inverse_one_ref[...], NT), inverse_two, NT)
    base_cols_ref[...] = ortho_cols + unit_rows(place_ref[1] * cols, cols, width)
    image_cols_ref[...] = dot(product_ref[...], band_inverse_t, NT) + edge_ref[...]


def split(x):
    high = x.astype(jnp.bfloat16)
    return high, (x - high.astype(jnp.float32)).astype(jnp.bfloat16)


def update_kernel(place_ref, trailing_ref, base_ref, image_ref, base_cols_ref, image_cols_ref, weight_ref, square_inverse_ref, upper_inverse_t_ref, updated_ref, reflectors_ref, high_ref, low_ref):
    rows, width = base_ref.shape
    step = pl.program_id(0)
    square_inverse = square_inverse_ref[...]
    weight = weight_ref[...]

    @pl.when(step == 0)
    def _():
        left = dot(base_cols_ref[...], square_inverse)
        right = image_cols_ref[...] - 0.5 * dot(left, weight)
        high_ref[...], low_ref[...] = split(jnp.concatenate([right, left], 1))

    base = base_ref[...]
    place = place_ref[0] * (rows * pl.num_programs(0)) + step * rows
    place = place + lax.broadcasted_iota(jnp.int32, (rows, width), 0)
    lane = lax.broadcasted_iota(jnp.int32, (rows, width), 1)
    reflectors = dot(base, upper_inverse_t_ref[...], NT)
    reflectors_ref[...] = jnp.where(place < lane, 0.0, jnp.where(place == lane, 1.0, reflectors))
    left = dot(base, square_inverse)
    right = image_ref[...] - 0.5 * dot(left, weight)
    high, low = split(jnp.concatenate([left, right], 1))
    change = dot(low, high_ref[...], NT, None) + dot(high, low_ref[...], NT, None)
    updated_ref[...] = trailing_ref[...] - (change + dot(high, high_ref[...], NT, None))


def update(place, trailing, base, image, base_cols, image_cols, weight, square_inverse, upper_inverse_t):
    rows, cols = trailing.shape
    width = base.shape[1]
    tile = rows // 8
    moving = lambda step: (step, 0)
    fixed = lambda step: (0, 0)
    range_spec = pl.BlockSpec((tile, width), moving)
    cols_spec = pl.BlockSpec((cols, width), fixed)
    square_spec = pl.BlockSpec((width, width), fixed)
    tile_spec = pl.BlockSpec((tile, cols), moving)
    return block_call(
        update_kernel,
        [(rows, cols), (rows, width)],
        "update",
        1 << 32,
        (place, trailing, base, image, base_cols, image_cols, weight, square_inverse, upper_inverse_t),
        grid=(rows // tile,),
        in_specs=[pl.BlockSpec(memory_space=pltpu.SMEM), tile_spec]
        + [range_spec] * 2
        + [cols_spec] * 2
        + [square_spec] * 3,
        out_specs=[tile_spec, range_spec],
        scratch_shapes=[pltpu.VMEM((cols, 2 * width), jnp.bfloat16)] * 2,
    )


def on_device(trailing, panel):
    rows, cols = trailing.shape
    chunk, width = panel.shape
    row_index = lax.axis_index("prow")
    col_index = lax.axis_index("pcol")
    chip, core = row_index // 2, row_index % 2
    y = col_index % YS
    place = jnp.stack([row_index, col_index]).astype(jnp.int32)
    scalars = pl.BlockSpec(memory_space=pltpu.SMEM)
    across_chips = lambda x, mask: swap_row(x, 2 * mask)

    edge = trailing[:width].T
    along_z = [panel] + [swap_z(panel, mask) for mask in range(1, ZS)]
    pair = lax.ppermute(edge, "prow", [(0, 1)])
    pair = jnp.where(row_index == 0, edge, pair)
    stack, pair = hold(jnp.concatenate(along_z, 0), pair)

    stacks = [stack] + [swap_y(stack, mask) for mask in range(1, YS)]
    arrived = [
        lax.ppermute(pair, "prow", [(0, 2 * far), (1, 2 * far + 1)]) for far in (1, 2, 3)
    ]
    (panel_rows,) = block_call(
        assemble_kernel, [(rows, width)], "assemble", 1 << 30, [place] + stacks,
        in_specs=[scalars] + whole(YS), out_specs=whole(1),
    )
    edge_cols = jnp.where(row_index < 2, pair, arrived[0] + arrived[1] + arrived[2])
    panel_rows, edge_cols = hold(panel_rows, edge_cols)

    gram = dot(panel_rows, panel_rows, TN)
    gram = gram + swap_row(gram, 1)
    product = dot(trailing, panel_rows, TN)
    leading = jnp.where(row_index == 0, panel_rows[:width], 0.0)
    payload = jnp.concatenate([product, leading], 0)
    edge_turned = transpose_chips(edge_cols)
    gram, payload, edge_turned = hold(gram, payload, edge_turned)

    half = payload.shape[0] // 2
    others = [across_chips(gram, mask) for mask in (1, 2, 3)]
    gram_one = (gram + others[0]) + (others[1] + others[2])
    other = swap_row(lax.dynamic_slice_in_dim(payload, (1 - core) * half, half, 0), 1)
    mine = lax.dynamic_slice_in_dim(payload, core * half, half, 0) + other
    panel_cols = transpose_chips(lax.dynamic_slice_in_dim(panel_rows, y * cols, cols, 0))
    gram_one, mine, panel_cols = hold(gram_one, mine, panel_cols)

    others = [across_chips(mine, mask) for mask in (1, 2, 3)]
    edges = [edge_turned] + [swap_y(edge_turned, mask) for mask in range(1, YS)]
    upper_one, inverse_one = small_call(first_kernel, 2, "first", gram_one)
    ortho_rows = dot(panel_rows, inverse_one, NT)
    gram = dot(ortho_rows, ortho_rows, TN)
    mine = (mine + others[0]) + (others[1] + others[2])
    gram, mine, *edges = hold(gram, mine, *edges)

    gram = gram + swap_row(gram, 1)
    other = swap_row(mine, 1)
    summed = jnp.where(
        core == 0, jnp.concatenate([mine, other], 0), jnp.concatenate([other, mine], 0)
    )
    gram, summed = hold(gram, summed)

    others = [across_chips(gram, mask) for mask in (1, 2, 3)]
    gram_two = (gram + others[0]) + (others[1] + others[2])
    product_cols, leading = summed[:cols], summed[cols:]
    product_turned = transpose_chips(product_cols)
    gram_two, product_turned = hold(gram_two, product_turned)

    products = [product_turned] + [swap_y(product_turned, mask) for mask in range(1, YS)]
    inverse_two, band_block, band_inverse_t, square = small_call(
        second_kernel, 4, "second", gram_two, upper_one, inverse_one, leading
    )
    base, image, weight, base_cols, image_cols = block_call(
        image_kernel,
        [(rows, width)] * 2 + [(width, width)] + [(cols, width)] * 2,
        "image",
        1 << 31,
        [place] + products + edges + [
            ortho_rows, panel_cols, product_cols, edge_cols, inverse_one, inverse_two, band_inverse_t
        ],
        in_specs=[scalars] + whole(2 * YS + 7),
        out_specs=whole(5),
    )

    weight = sum_rows(weight)
    factor, upper_inverse_t, square_inverse = small_call(third_kernel, 3, "third", square)
    updated, reflectors = update(
        place, trailing, base, image, base_cols, image_cols, weight, square_inverse, upper_inverse_t
    )
    return (updated, reflectors, factor, band_block, upper_one)


def solution(mesh):
    placed = (P("prow", "pcol"), P(("prow", "pcol"), None))
    return jax.shard_map(
        on_device,
        mesh=mesh,
        in_specs=placed,
        out_specs=(P("prow", "pcol"), P("prow", None), P(), P(), P()),
        check_vma=False,
    )
```

```python
import functools

import jax
import jax.numpy as jnp
from jax import lax
from jax.experimental import pallas as pl
from jax.experimental.pallas import tpu as pltpu
from jax.sharding import PartitionSpec as P

HIGHEST = lax.Precision.HIGHEST
ROWS, ZS, YS = 8, 8, 4
NN = (((1,), (0,)), ((), ()))
NT = (((1,), (1,)), ((), ()))
TN = (((0,), (0,)), ((), ()))


def dot(left, right, dims=NN, precision=HIGHEST):
    return lax.dot_general(
        left, right, dims, precision=precision, preferred_element_type=jnp.float32
    )


def recip(x):
    r = pl.reciprocal(x, approx=True)
    r = r * (2.0 - x * r)
    return r * (2.0 - x * r)


def eliminate(mats):
    n = mats[0].shape[0]
    lane = lax.broadcasted_iota(jnp.int32, (8, n), 1)
    sub = lax.broadcasted_iota(jnp.int32, (8, n), 0)
    across = lambda x, k: jnp.broadcast_to(x[:, k : k + 1], (8, n))
    down = lambda x, s: jnp.broadcast_to(x[s : s + 1], (8, n))
    tiles = [[m[8 * t : 8 * t + 8] for t in range(n // 8)] for m in mats]
    for t in range(n // 8):
        base = 8 * t
        block = (lane >= base) & (lane < base + 8)
        for m in tiles:
            cols = [across(m[t], base + s) for s in range(8)]
            work = m[t]
            invs, rows, heads = [], [], []
            for s in range(8):
                here = lane == base + s
                below = sub > s
                inv = recip(down(cols[s], s))
                row = jnp.where(here, 1.0, down(work, s))
                mult = jnp.where(below, cols[s] * inv, 0.0)
                work = jnp.where(here & below, 0.0, work) - mult * row
                head = [down(cols[q], s) for q in range(s + 1, 8)]
                for q in range(s + 1, 8):
                    cols[q] = cols[q] - mult * head[q - s - 1]
                invs.append(inv)
                rows.append(jnp.where(block & (lane > base + s), 0.0, row))
                heads.append(head)
            m[t] = work
            for j in range(t + 1, n // 8):
                cols = [across(m[j], base + s) for s in range(8)]
                new = jnp.where(block, 0.0, m[j])
                for s in range(8):
                    mult = cols[s] * invs[s]
                    new = new - mult * rows[s]
                    for q in range(s + 1, 8):
                        cols[q] = cols[q] - mult * heads[s][q - s - 1]
                m[j] = new
    return [jnp.concatenate(m, 0) for m in tiles]


def positions(n):
    row = lax.broadcasted_iota(jnp.int32, (n, n), 0)
    col = lax.broadcasted_iota(jnp.int32, (n, n), 1)
    return row, col


def cholesky_pair(gram):
    (packed,) = eliminate([gram])
    row, col = positions(gram.shape[0])
    pivots = jnp.sum(jnp.where(row == col, packed, 0.0), 1, keepdims=True)
    scale = 1.0 / jnp.sqrt(pivots)
    upper = jnp.where(col >= row, packed, 0.0) * scale
    inverse = jnp.where(col < row, packed, jnp.where(col == row, 1.0, 0.0)) * scale
    return upper, inverse


def split(x):
    high = x.astype(jnp.bfloat16)
    return high, (x - high.astype(jnp.float32)).astype(jnp.bfloat16)


def dot_split(left, right, dims=NN):
    small = dot(left[1], right[0], dims, None) + dot(left[0], right[1], dims, None)
    return small + dot(left[0], right[0], dims, None)


def four_sum(refs):
    one, two, three, four = (ref[...] for ref in refs)
    return (one + two) + (three + four)


def product_kernel(place_ref, panel_ref, trailing_ref, gram_ref, payload_ref, total_ref):
    step = pl.program_id(0)
    cols, width = trailing_ref.shape[1], panel_ref.shape[1]
    panel = panel_ref[...]
    gram = dot(panel, panel, TN)
    total = dot(panel, trailing_ref[...], TN)

    @pl.when(step == 0)
    def _():
        gram_ref[...] = gram
        total_ref[...] = total
        payload_ref[cols:, :] = jnp.where(place_ref[0] == 0, panel[:width], 0.0)

    @pl.when(step > 0)
    def _():
        gram_ref[...] += gram
        total_ref[...] += total

    @pl.when(step == pl.num_programs(0) - 1)
    def _():
        payload_ref[:cols, :] = total_ref[...].T


def first_kernel(*refs):
    panel_ref, upper_ref, inverse_ref, ortho_ref, gram_ref = refs[4:]
    upper_ref[...], inverse = cholesky_pair(four_sum(refs[:4]))
    inverse_ref[...] = inverse
    ortho = dot(panel_ref[...], inverse, NT)
    ortho_ref[...] = ortho
    gram_ref[...] = dot(ortho, ortho, TN)


def second_kernel(*refs):
    upper_one_ref, inverse_one_ref, leading_ref = refs[4:7]
    inverse_two_ref, band_ref, band_inverse_t_ref, square_ref = refs[7:]
    upper, inverse = cholesky_pair(four_sum(refs[:4]))
    row, col = positions(upper.shape[0])
    inverse_one = inverse_one_ref[...]
    inverse_two_ref[...] = inverse
    band_ref[...] = dot(upper, upper_one_ref[...])
    band_inverse_t_ref[...] = dot(inverse, inverse_one)
    top = dot(dot(leading_ref[...], inverse_one, NT), inverse, NT)
    square_ref[...] = top + jnp.where(row == col, 1.0, 0.0)


def third_kernel(square_ref, factor_ref, upper_inverse_ref, square_inverse_ref):
    square = square_ref[...]
    one, two = eliminate([square, square.T])
    row, col = positions(square.shape[0])
    unit = jnp.where(row == col, 1.0, 0.0)
    pivots = jnp.sum(jnp.where(row == col, two, 0.0), 1, keepdims=True)
    upper = jnp.where(col >= row, one, 0.0)
    lower_inverse = jnp.where(col < row, one, unit)
    upper_inverse = (jnp.where(col < row, two, unit) / pivots).T
    factor_ref[...] = dot(upper, lower_inverse, NT)
    upper_inverse_ref[...] = upper_inverse
    square_inverse_ref[...] = dot(upper_inverse, lower_inverse)


def block_call(body, outs, name, cost, args, **more):
    return pl.pallas_call(
        body,
        out_shape=[jax.ShapeDtypeStruct(shape, jnp.float32) for shape in outs],
        name=name,
        cost_estimate=pl.CostEstimate(flops=cost, bytes_accessed=1 << 20, transcendentals=0),
        compiler_params=pltpu.CompilerParams(vmem_limit_bytes=40 << 20),
        **more,
    )(*args)


def whole(count):
    return [pl.BlockSpec(memory_space=pltpu.VMEM)] * count


def scalars():
    return pl.BlockSpec(memory_space=pltpu.SMEM)


def assemble_kernel(place_ref, *refs):
    stacks, out_ref = refs[:-1], refs[-1]
    chunk = stacks[0].shape[1]
    y = place_ref[1] % YS
    for far, stack in enumerate(stacks):
        for z in range(ZS):
            at = (z * YS + (y ^ far)) * chunk
            out_ref[pl.ds(pl.multiple_of(at, chunk), chunk), :] = stack[z]


def unit_rows(start, count, width):
    place = start + lax.broadcasted_iota(jnp.int32, (count, width), 0)
    return jnp.where(place == lax.broadcasted_iota(jnp.int32, (count, width), 1), 1.0, 0.0)


def image_kernel(place_ref, *refs):
    products, edges = refs[:YS], refs[YS : 2 * YS]
    ortho_ref, panel_ref, product_ref, edge_ref, inverse_one_ref, inverse_two_ref, band_inverse_t_ref = refs[2 * YS : 2 * YS + 7]
    base_ref, image_ref, weight_ref, base_cols_ref, image_cols_ref = refs[2 * YS + 7 :]
    cols, width = products[0].shape
    y = place_ref[1] % YS
    inverse_two = split(inverse_two_ref[...])
    band_inverse_t = band_inverse_t_ref[...]
    weight = jnp.zeros((width, width), jnp.float32)
    for far in range(YS):
        at = pl.multiple_of((y ^ far) * cols, cols)
        span = pl.ds(at, cols)
        start = place_ref[0] * (YS * cols) + at
        base = dot_split(split(ortho_ref[span, :]), inverse_two, NT) + unit_rows(start, cols, width)
        image = dot(products[far][...], band_inverse_t, NT) + edges[far][...]
        base_ref[span, :] = base
        image_ref[span, :] = image
        weight = weight + dot_split(split(base), split(image), TN)
    weight_ref[...] = weight
    ortho_cols = dot_split(split(dot(panel_ref[...], inverse_one_ref[...], NT)), inverse_two, NT)
    base_cols_ref[...] = ortho_cols + unit_rows(place_ref[1] * cols, cols, width)
    image_cols_ref[...] = dot(product_ref[...], band_inverse_t, NT) + edge_ref[...]


def update_kernel(place_ref, *refs):
    weights = refs[:4]
    trailing_ref, base_ref, image_ref, base_cols_ref, image_cols_ref, square_inverse_ref, upper_inverse_ref = refs[4:11]
    updated_ref, reflectors_ref, high_ref, low_ref, right_high_ref, right_low_ref = refs[11:]
    rows, width = base_ref.shape
    step = pl.program_id(0)

    @pl.when(step == 0)
    def _():
        square_inverse = square_inverse_ref[...]
        halved = 0.5 * dot(square_inverse, four_sum(weights))
        table = split(jnp.concatenate([square_inverse, halved, upper_inverse_ref[...]], 1))
        right_high_ref[...], right_low_ref[...] = table
        left = dot_split(split(base_cols_ref[...]), (table[0][:, : 2 * width], table[1][:, : 2 * width]))
        right = image_cols_ref[...] - left[:, width:]
        high_ref[...], low_ref[...] = split(jnp.concatenate([right, left[:, :width]], 1))

    left = dot_split(split(base_ref[...]), (right_high_ref[...], right_low_ref[...]))
    right = image_ref[...] - left[:, width : 2 * width]
    pair = split(jnp.concatenate([left[:, :width], right], 1))
    updated_ref[...] = trailing_ref[...] - dot_split(pair, (high_ref[...], low_ref[...]), NT)
    place = place_ref[0] * (rows * pl.num_programs(0)) + step * rows
    place = place + lax.broadcasted_iota(jnp.int32, (rows, width), 0)
    lane = lax.broadcasted_iota(jnp.int32, (rows, width), 1)
    reflectors = left[:, 2 * width :]
    reflectors_ref[...] = jnp.where(place < lane, 0.0, jnp.where(place == lane, 1.0, reflectors))


def update(place, weights, trailing, base, image, base_cols, image_cols, square_inverse, upper_inverse, steps=8):
    rows, cols = trailing.shape
    width = base.shape[1]
    tile = rows // steps
    moving = lambda step: (step, 0)
    fixed = lambda step: (0, 0)
    range_spec = pl.BlockSpec((tile, width), moving)
    cols_spec = pl.BlockSpec((cols, width), fixed)
    square_spec = pl.BlockSpec((width, width), fixed)
    tile_spec = pl.BlockSpec((tile, cols), moving)
    return block_call(
        update_kernel,
        [(rows, cols), (rows, width)],
        "update",
        1 << 32,
        [place, *weights, trailing, base, image, base_cols, image_cols, square_inverse, upper_inverse],
        grid=(steps,),
        in_specs=[scalars()] + [square_spec] * 4 + [tile_spec] + [range_spec] * 2
        + [cols_spec] * 2 + [square_spec] * 2,
        out_specs=[tile_spec, range_spec],
        scratch_shapes=[pltpu.VMEM((cols, 2 * width), jnp.bfloat16)] * 2
        + [pltpu.VMEM((width, 3 * width), jnp.bfloat16)] * 2,
    )


def products(place, panel, trailing, steps=4):
    rows, cols = trailing.shape
    width = panel.shape[1]
    tile = rows // steps
    moving = lambda step: (step, 0)
    fixed = lambda step: (0, 0)
    return block_call(
        product_kernel,
        [(width, width), (cols + width, width)],
        "products",
        1 << 31,
        [place, panel, trailing],
        grid=(steps,),
        in_specs=[scalars(), pl.BlockSpec((tile, width), moving), pl.BlockSpec((tile, cols), moving)],
        out_specs=[pl.BlockSpec((width, width), fixed), pl.BlockSpec((cols + width, width), fixed)],
        scratch_shapes=[pltpu.VMEM((width, cols), jnp.float32)],
    )


def swap_row(x, mask):
    return lax.ppermute(x, "prow", [(r, r ^ mask) for r in range(ROWS)])


def swap_y(x, mask):
    return lax.ppermute(x, "pcol", [(c, c ^ mask) for c in range(ZS * YS)])


def turn_z(x):
    pairs = [(r, z, z ^ (r // 2 + 4 * (r % 2))) for r in range(ROWS) for z in range(ZS)]
    return lax.ppermute(x, ("prow", "pcol"), [(place_of(r, z, y), place_of(r, t, y)) for r, z, t in pairs for y in range(YS)])


def turn_row(x, back=False):
    pairs = [(r, z, z ^ (r // 2 + 4 * (r % 2))) for r in range(ROWS) for z in range(ZS)]
    moves = [(place_of(r, z, y), place_of(t, z, y)) for r, z, t in pairs for y in range(YS)]
    if back:
        moves = [(t, f) for f, t in moves]
    return lax.ppermute(x, ("prow", "pcol"), moves)


def place_of(r, z, y):
    return (r * ZS + z) * YS + y


def three_rows(x):
    return [x] + [swap_row(x, 2 * mask) for mask in (1, 2, 3)]


def along_y(x):
    return [x] + [swap_y(x, mask) for mask in range(1, YS)]


def hold(*arrays):
    return lax.optimization_barrier(arrays)


def on_device(trailing, panel):
    rows, cols = trailing.shape
    chunk, width = panel.shape
    square = (width, width)
    row_index = lax.axis_index("prow")
    col_index = lax.axis_index("pcol")
    core = row_index % 2
    y = col_index % YS
    place = jnp.stack([row_index, col_index]).astype(jnp.int32)

    edge = trailing[:width].T
    pair = lax.ppermute(edge, "prow", [(0, 1)])
    pair = jnp.where(row_index == 0, edge, pair)
    lines = [[z * YS + at for z in range(ZS)] for at in range(YS)]
    copies = jnp.broadcast_to(panel[None], (ZS, chunk, width))
    stack = lax.all_to_all(copies, "pcol", 0, 0, axis_index_groups=lines)
    stack, pair = hold(stack, pair)

    arrived = [
        lax.ppermute(pair, "prow", [(0, 2 * far), (1, 2 * far + 1)]) for far in (1, 2, 3)
    ]
    (panel_rows,) = block_call(
        assemble_kernel, [(rows, width)], "assemble", 1 << 30, [place] + along_y(stack),
        in_specs=[scalars()] + whole(YS), out_specs=whole(1),
    )

    gram, payload = products(place, panel_rows, trailing)
    gram = gram + swap_row(gram, 1)
    half = payload.shape[0] // 2
    other = swap_row(lax.dynamic_slice_in_dim(payload, (1 - core) * half, half, 0), 1)
    mine = lax.dynamic_slice_in_dim(payload, core * half, half, 0) + other
    edge_cols = jnp.where(row_index < 2, pair, arrived[0] + arrived[1] + arrived[2])
    gram, mine, edge_cols = hold(gram, mine, edge_cols)

    grams = three_rows(gram)
    one, two, three, four = three_rows(mine)
    mine = (one + two) + (three + four)
    edge_turned = turn_z(edge_cols)
    panel_cols = lax.dynamic_slice_in_dim(panel_rows, y * cols, cols, 0)
    panel_cols = turn_row(panel_cols, back=True)
    *grams, mine, edge_turned, panel_cols = hold(*grams, mine, edge_turned, panel_cols)

    other = swap_row(mine, 1)
    summed = jnp.where(
        core == 0, jnp.concatenate([mine, other], 0), jnp.concatenate([other, mine], 0)
    )
    product_cols, leading = summed[:cols], summed[cols:]
    product_turned = turn_z(product_cols)
    edge_turned = turn_row(edge_turned)
    upper_one, inverse_one, ortho_rows, gram = block_call(
        first_kernel, [square, square, (rows, width), square], "first", 1 << 33, grams + [panel_rows],
        in_specs=whole(5), out_specs=whole(4),
    )
    gram, product_turned, edge_turned = hold(gram, product_turned, edge_turned)

    gram = gram + swap_row(gram, 1)
    product_turned = turn_row(product_turned)
    grams = three_rows(gram)
    edges = along_y(edge_turned)
    *grams, product_turned = hold(*grams, product_turned)

    panel_cols = turn_z(panel_cols)
    turned = along_y(product_turned)
    inverse_two, band_block, band_inverse_t, top = block_call(
        second_kernel, [square] * 4, "second", 1 << 33, grams + [upper_one, inverse_one, leading],
        in_specs=whole(7), out_specs=whole(4),
    )
    factor, upper_inverse, square_inverse = block_call(
        third_kernel, [square] * 3, "third", 1 << 33, [top], in_specs=whole(1), out_specs=whole(3)
    )
    base, image, weight, base_cols, image_cols = block_call(
        image_kernel,
        [(rows, width)] * 2 + [square] + [(cols, width)] * 2,
        "image",
        1 << 31,
        [place] + turned + edges + [
            ortho_rows, panel_cols, product_cols, edge_cols, inverse_one, inverse_two, band_inverse_t
        ],
        in_specs=[scalars()] + whole(2 * YS + 7),
        out_specs=whole(5),
    )

    weights = three_rows(weight + swap_row(weight, 1))
    updated, reflectors = update(
        place, weights, trailing, base, image, base_cols, image_cols, square_inverse, upper_inverse
    )
    return (updated, reflectors, factor, band_block, upper_one)


def solution(mesh):
    placed = (P("prow", "pcol"), P(("prow", "pcol"), None))
    return jax.shard_map(
        on_device,
        mesh=mesh,
        in_specs=placed,
        out_specs=(P("prow", "pcol"), P("prow", None), P(), P(), P()),
        check_vma=False,
    )
```

```python
import functools

import jax
import jax.numpy as jnp
from jax import lax
from jax.experimental import pallas as pl
from jax.experimental.pallas import tpu as pltpu
from jax.sharding import PartitionSpec as P

HIGHEST = lax.Precision.HIGHEST
ROWS, ZS, YS = 8, 8, 4
PARTS = 4
NN = (((1,), (0,)), ((), ()))
NT = (((1,), (1,)), ((), ()))
TN = (((0,), (0,)), ((), ()))


def dot(left, right, dims=NN, precision=HIGHEST):
    return lax.dot_general(
        left, right, dims, precision=precision, preferred_element_type=jnp.float32
    )


def recip(x):
    r = pl.reciprocal(x, approx=True)
    r = r * (2.0 - x * r)
    return r * (2.0 - x * r)


def eliminate(mats):
    n = mats[0].shape[0]
    lane = lax.broadcasted_iota(jnp.int32, (8, n), 1)
    sub = lax.broadcasted_iota(jnp.int32, (8, n), 0)
    across = lambda x, k: jnp.broadcast_to(x[:, k : k + 1], (8, n))
    down = lambda x, s: jnp.broadcast_to(x[s : s + 1], (8, n))
    tiles = [[m[8 * t : 8 * t + 8] for t in range(n // 8)] for m in mats]
    for t in range(n // 8):
        base = 8 * t
        block = (lane >= base) & (lane < base + 8)
        for m in tiles:
            cols = [across(m[t], base + s) for s in range(8)]
            work = m[t]
            invs, rows, heads = [], [], []
            for s in range(8):
                here = lane == base + s
                below = sub > s
                inv = recip(down(cols[s], s))
                row = jnp.where(here, 1.0, down(work, s))
                mult = jnp.where(below, cols[s] * inv, 0.0)
                work = jnp.where(here & below, 0.0, work) - mult * row
                head = [down(cols[q], s) for q in range(s + 1, 8)]
                for q in range(s + 1, 8):
                    cols[q] = cols[q] - mult * head[q - s - 1]
                invs.append(inv)
                rows.append(jnp.where(block & (lane > base + s), 0.0, row))
                heads.append(head)
            m[t] = work
            for j in range(t + 1, n // 8):
                cols = [across(m[j], base + s) for s in range(8)]
                new = jnp.where(block, 0.0, m[j])
                for s in range(8):
                    mult = cols[s] * invs[s]
                    new = new - mult * rows[s]
                    for q in range(s + 1, 8):
                        cols[q] = cols[q] - mult * heads[s][q - s - 1]
                m[j] = new
    return [jnp.concatenate(m, 0) for m in tiles]


def positions(n):
    row = lax.broadcasted_iota(jnp.int32, (n, n), 0)
    col = lax.broadcasted_iota(jnp.int32, (n, n), 1)
    return row, col


def cholesky_pair(gram):
    (packed,) = eliminate([gram])
    row, col = positions(gram.shape[0])
    pivots = jnp.sum(jnp.where(row == col, packed, 0.0), 1, keepdims=True)
    scale = 1.0 / jnp.sqrt(pivots)
    upper = jnp.where(col >= row, packed, 0.0) * scale
    inverse = jnp.where(col < row, packed, jnp.where(col == row, 1.0, 0.0)) * scale
    return upper, inverse


def split(x):
    high = x.astype(jnp.bfloat16)
    return high, (x - high.astype(jnp.float32)).astype(jnp.bfloat16)


def dot_split(left, right, dims=NN):
    small = dot(left[1], right[0], dims, None) + dot(left[0], right[1], dims, None)
    return small + dot(left[0], right[0], dims, None)


def four_sum(refs):
    one, two, three, four = (ref[...] for ref in refs)
    return (one + two) + (three + four)


def panel_kernel(place_ref, *refs):
    stacks, (trailing_ref, panel_ref, gram_ref, payload_ref, copy_ref, sems) = refs[:YS], refs[YS:]
    rows, cols = trailing_ref.shape
    chunk, width = stacks[0].shape[1:]
    tile = rows // PARTS
    copies = []
    for part in range(PARTS):
        span = pl.ds(part * tile, tile)
        copies.append(pltpu.make_async_copy(trailing_ref.at[span, :], copy_ref.at[span, :], sems.at[part]))
        copies[-1].start()
    y = place_ref[1] % YS
    for far, stack in enumerate(stacks):
        for z in range(ZS):
            at = (z * YS + (y ^ far)) * chunk
            panel_ref[pl.ds(pl.multiple_of(at, chunk), chunk), :] = stack[z]
    panel = panel_ref[...]
    gram_ref[...] = dot(panel, panel, TN)
    total = jnp.zeros((width, cols), jnp.float32)
    for part in range(PARTS):
        copies[part].wait()
        span = slice(part * tile, (part + 1) * tile)
        total = total + dot(panel[span], copy_ref[span, :], TN)
    payload_ref[:cols, :] = total.T
    payload_ref[cols:, :] = jnp.where(place_ref[0] == 0, panel[:width], 0.0)


def first_kernel(*refs):
    panel_ref, upper_ref, inverse_ref, ortho_ref, gram_ref = refs[4:]
    width = panel_ref.shape[1]
    upper_ref[...], inverse = cholesky_pair(four_sum([ref.at[:width] for ref in refs[:4]]))
    inverse_ref[...] = inverse
    ortho = dot(panel_ref[...], inverse, NT)
    ortho_ref[...] = ortho
    gram_ref[...] = dot(ortho, ortho, TN)


def second_kernel(*refs):
    upper_one_ref, inverse_one_ref, leading_ref = refs[4:7]
    inverse_two_ref, band_ref, band_inverse_t_ref, square_ref = refs[7:]
    upper, inverse = cholesky_pair(four_sum(refs[:4]))
    row, col = positions(upper.shape[0])
    inverse_one = inverse_one_ref[...]
    inverse_two_ref[...] = inverse
    band_ref[...] = dot(upper, upper_one_ref[...])
    band_inverse_t_ref[...] = dot(inverse, inverse_one)
    top = dot(dot(leading_ref[...], inverse_one, NT), inverse, NT)
    square_ref[...] = top + jnp.where(row == col, 1.0, 0.0)


def third_kernel(square_ref, factor_ref, upper_inverse_ref, square_inverse_ref):
    square = square_ref[...]
    one, two = eliminate([square, square.T])
    row, col = positions(square.shape[0])
    unit = jnp.where(row == col, 1.0, 0.0)
    pivots = jnp.sum(jnp.where(row == col, two, 0.0), 1, keepdims=True)
    upper = jnp.where(col >= row, one, 0.0)
    lower_inverse = jnp.where(col < row, one, unit)
    upper_inverse = (jnp.where(col < row, two, unit) / pivots).T
    factor_ref[...] = dot(upper, lower_inverse, NT)
    upper_inverse_ref[...] = upper_inverse
    square_inverse_ref[...] = dot(upper_inverse, lower_inverse)


def block_call(body, outs, name, cost, args, room=40, **more):
    return pl.pallas_call(
        body,
        out_shape=[jax.ShapeDtypeStruct(shape, jnp.float32) for shape in outs],
        name=name,
        cost_estimate=pl.CostEstimate(flops=cost, bytes_accessed=1 << 20, transcendentals=0),
        compiler_params=pltpu.CompilerParams(vmem_limit_bytes=room << 20),
        **more,
    )(*args)


def whole(count):
    return [pl.BlockSpec(memory_space=pltpu.VMEM)] * count


def scalars():
    return pl.BlockSpec(memory_space=pltpu.SMEM)


def unit_rows(start, count, width):
    place = start + lax.broadcasted_iota(jnp.int32, (count, width), 0)
    return jnp.where(place == lax.broadcasted_iota(jnp.int32, (count, width), 1), 1.0, 0.0)


def image_kernel(place_ref, *refs):
    products, edges = refs[:YS], refs[YS : YS + 2]
    ortho_ref, panel_ref, product_ref, edge_ref, inverse_one_ref, inverse_two_ref, band_inverse_t_ref = refs[YS + 2 : YS + 9]
    base_ref, image_ref, weight_ref, base_cols_ref, image_cols_ref = refs[YS + 9 :]
    cols, width = products[0].shape
    y = place_ref[1] % YS
    inverse_two = split(inverse_two_ref[...])
    band_inverse_t = band_inverse_t_ref[...]
    weight = jnp.zeros((width, width), jnp.float32)
    for far in range(YS):
        at = pl.multiple_of((y ^ far) * cols, cols)
        span = pl.ds(at, cols)
        start = place_ref[0] * (YS * cols) + at
        base = dot_split(split(ortho_ref[span, :]), inverse_two, NT) + unit_rows(start, cols, width)
        image = dot(products[far][...], band_inverse_t, NT) + edges[far // 2][(far % 2) * cols : (far % 2 + 1) * cols, :]
        base_ref[span, :] = base
        image_ref[span, :] = image
        weight = weight + dot_split(split(base), split(image), TN)
    weight_ref[...] = weight
    ortho_cols = dot_split(split(dot(panel_ref[...], inverse_one_ref[...], NT)), inverse_two, NT)
    base_cols_ref[...] = ortho_cols + unit_rows(place_ref[1] * cols, cols, width)
    image_cols_ref[...] = dot(product_ref[...], band_inverse_t, NT) + edge_ref[...]


def update_kernel(place_ref, *refs):
    weights = refs[:4]
    trailing_ref, base_ref, image_ref, base_cols_ref, image_cols_ref, square_inverse_ref, upper_inverse_ref = refs[4:11]
    updated_ref, reflectors_ref, high_ref, low_ref, right_high_ref, right_low_ref = refs[11:]
    rows, width = base_ref.shape
    step = pl.program_id(0)

    @pl.when(step == 0)
    def _():
        square_inverse = square_inverse_ref[...]
        halved = 0.5 * dot(square_inverse, four_sum(weights))
        table = split(jnp.concatenate([square_inverse, halved, upper_inverse_ref[...]], 1))
        right_high_ref[...], right_low_ref[...] = table
        left = dot_split(split(base_cols_ref[...]), (table[0][:, : 2 * width], table[1][:, : 2 * width]))
        right = image_cols_ref[...] - left[:, width:]
        high_ref[...], low_ref[...] = split(jnp.concatenate([right, left[:, :width]], 1))

    left = dot_split(split(base_ref[...]), (right_high_ref[...], right_low_ref[...]))
    right = image_ref[...] - left[:, width : 2 * width]
    pair = split(jnp.concatenate([left[:, :width], right], 1))
    updated_ref[...] = trailing_ref[...] - dot_split(pair, (high_ref[...], low_ref[...]), NT)
    place = place_ref[0] * (rows * pl.num_programs(0)) + step * rows
    place = place + lax.broadcasted_iota(jnp.int32, (rows, width), 0)
    lane = lax.broadcasted_iota(jnp.int32, (rows, width), 1)
    reflectors = left[:, 2 * width :]
    reflectors_ref[...] = jnp.where(place < lane, 0.0, jnp.where(place == lane, 1.0, reflectors))


def update(place, weights, trailing, base, image, base_cols, image_cols, square_inverse, upper_inverse, steps=8):
    rows, cols = trailing.shape
    width = base.shape[1]
    tile = rows // steps
    moving = lambda step: (step, 0)
    fixed = lambda step: (0, 0)
    range_spec = pl.BlockSpec((tile, width), moving)
    cols_spec = pl.BlockSpec((cols, width), fixed)
    square_spec = pl.BlockSpec((width, width), fixed)
    tile_spec = pl.BlockSpec((tile, cols), moving)
    return block_call(
        update_kernel,
        [(rows, cols), (rows, width)],
        "update",
        1 << 32,
        [place, *weights, trailing, base, image, base_cols, image_cols, square_inverse, upper_inverse],
        grid=(steps,),
        in_specs=[scalars()] + [square_spec] * 4 + [tile_spec] + [range_spec] * 2
        + [cols_spec] * 2 + [square_spec] * 2,
        out_specs=[tile_spec, range_spec],
        scratch_shapes=[pltpu.VMEM((cols, 2 * width), jnp.bfloat16)] * 2
        + [pltpu.VMEM((width, 3 * width), jnp.bfloat16)] * 2,
    )


def swap_row(x, mask):
    return lax.ppermute(x, "prow", [(r, r ^ mask) for r in range(ROWS)])


def swap_y(x, mask):
    return lax.ppermute(x, "pcol", [(c, c ^ mask) for c in range(ZS * YS)])


def turn_z(x):
    pairs = [(r, z, z ^ (r // 2 + 4 * (r % 2))) for r in range(ROWS) for z in range(ZS)]
    return lax.ppermute(x, ("prow", "pcol"), [(place_of(r, z, y), place_of(r, t, y)) for r, z, t in pairs for y in range(YS)])


def turn_row(x, back=False):
    pairs = [(r, z, z ^ (r // 2 + 4 * (r % 2))) for r in range(ROWS) for z in range(ZS)]
    moves = [(place_of(r, z, y), place_of(t, z, y)) for r, z, t in pairs for y in range(YS)]
    if back:
        moves = [(t, f) for f, t in moves]
    return lax.ppermute(x, ("prow", "pcol"), moves)


def place_of(r, z, y):
    return (r * ZS + z) * YS + y


def three_rows(x):
    return [x] + [swap_row(x, 2 * mask) for mask in (1, 2, 3)]


def along_y(x):
    return [x] + [swap_y(x, mask) for mask in range(1, YS)]


def hold(*arrays):
    return lax.optimization_barrier(arrays)


def on_device(trailing, panel):
    rows, cols = trailing.shape
    chunk, width = panel.shape
    square = (width, width)
    row_index = lax.axis_index("prow")
    col_index = lax.axis_index("pcol")
    core = row_index % 2
    y = col_index % YS
    place = jnp.stack([row_index, col_index]).astype(jnp.int32)

    lines = [[z * YS + at for z in range(ZS)] for at in range(YS)]
    copies = jnp.broadcast_to(panel[None], (ZS, chunk, width))
    source, copies = hold(trailing[:width], copies)
    stack = lax.all_to_all(copies, "pcol", 0, 0, axis_index_groups=lines)
    edge = source.T
    pair = lax.ppermute(edge, "prow", [(0, 1)])
    pair = jnp.where(row_index == 0, edge, pair)
    arrived = [
        lax.ppermute(pair, "prow", [(0, 2 * far), (1, 2 * far + 1)]) for far in (1, 2, 3)
    ]
    edge_cols = jnp.where(row_index < 2, pair, arrived[0] + arrived[1] + arrived[2])

    edge_turned = turn_z(edge_cols)
    panel_rows, gram, payload = block_call(
        panel_kernel,
        [(rows, width), square, (cols + width, width)],
        "panel",
        1 << 32,
        [place] + along_y(stack) + [trailing],
        room=58,
        in_specs=[scalars()] + whole(YS) + [pl.BlockSpec(memory_space=pltpu.HBM)],
        out_specs=whole(3),
        scratch_shapes=[pltpu.VMEM((rows, cols), jnp.float32), pltpu.SemaphoreType.DMA((PARTS,))],
    )
    panel_rows, gram, payload, edge_turned = hold(panel_rows, gram, payload, edge_turned)

    edge_turned = turn_row(edge_turned)
    half = payload.shape[0] // 2
    away = lax.dynamic_slice_in_dim(payload, (1 - core) * half, half, 0)
    mine = lax.dynamic_slice_in_dim(payload, core * half, half, 0)
    message = jnp.concatenate([gram, mine], 0)
    message = message + swap_row(jnp.concatenate([gram, away], 0), 1)
    message, edge_turned = hold(message, edge_turned)
    messages = three_rows(message)
    edge_pair = jnp.concatenate([edge_turned, swap_y(edge_turned, 1)], 0)
    *messages, edge_pair = hold(*messages, edge_pair)

    mine = (messages[0][width:] + messages[1][width:]) + (messages[2][width:] + messages[3][width:])
    other = swap_row(mine, 1)
    summed = jnp.where(
        core == 0, jnp.concatenate([mine, other], 0), jnp.concatenate([other, mine], 0)
    )
    *messages, summed = hold(*messages, summed)
    product_cols, leading = summed[:cols], summed[cols:]
    product_turned = turn_z(product_cols)
    panel_cols = turn_row(lax.dynamic_slice_in_dim(panel_rows, y * cols, cols, 0), back=True)
    upper_one, inverse_one, ortho_rows, gram = block_call(
        first_kernel, [square, square, (rows, width), square], "first", 1 << 33, messages + [panel_rows],
        in_specs=whole(5), out_specs=whole(4),
    )
    gram, product_turned, panel_cols = hold(gram, product_turned, panel_cols)

    gram = gram + swap_row(gram, 1)
    product_turned = turn_row(product_turned)
    grams = three_rows(gram)
    *grams, product_turned = hold(*grams, product_turned)

    turned = along_y(product_turned)
    panel_cols = turn_z(panel_cols)
    edges = [edge_pair, swap_y(edge_pair, 2)]
    inverse_two, band_block, band_inverse_t, top = block_call(
        second_kernel, [square] * 4, "second", 1 << 33, grams + [upper_one, inverse_one, leading],
        in_specs=whole(7), out_specs=whole(4),
    )
    factor, upper_inverse, square_inverse = block_call(
        third_kernel, [square] * 3, "third", 1 << 33, [top], in_specs=whole(1), out_specs=whole(3)
    )
    square_inverse, *turned = hold(square_inverse, *turned)
    base, image, weight, base_cols, image_cols = block_call(
        image_kernel,
        [(rows, width)] * 2 + [square] + [(cols, width)] * 2,
        "image",
        1 << 31,
        [place] + turned + edges + [
            ortho_rows, panel_cols, product_cols, edge_cols, inverse_one, inverse_two, band_inverse_t
        ],
        in_specs=[scalars()] + whole(YS + 9),
        out_specs=whole(5),
    )

    weights = three_rows(weight + swap_row(weight, 1))
    updated, reflectors = update(
        place, weights, trailing, base, image, base_cols, image_cols, square_inverse, upper_inverse
    )
    return (updated, reflectors, factor, band_block, upper_one)


def solution(mesh):
    placed = (P("prow", "pcol"), P(("prow", "pcol"), None))
    return jax.shard_map(
        on_device,
        mesh=mesh,
        in_specs=placed,
        out_specs=(P("prow", "pcol"), P("prow", None), P(), P(), P()),
        check_vma=False,
    )
```

```python
import functools

import jax
import jax.numpy as jnp
from jax import lax
from jax.experimental import pallas as pl
from jax.experimental.pallas import tpu as pltpu
from jax.sharding import PartitionSpec as P

HIGHEST = lax.Precision.HIGHEST
ROWS, ZS, YS = 8, 8, 4
PARTS = 4
NN = (((1,), (0,)), ((), ()))
NT = (((1,), (1,)), ((), ()))
TN = (((0,), (0,)), ((), ()))


def dot(left, right, dims=NN, precision=HIGHEST):
    return lax.dot_general(
        left, right, dims, precision=precision, preferred_element_type=jnp.float32
    )


def recip(x):
    r = pl.reciprocal(x, approx=True)
    r = r * (2.0 - x * r)
    return r * (2.0 - x * r)


def eliminate(mats):
    n = mats[0].shape[0]
    lane = lax.broadcasted_iota(jnp.int32, (8, n), 1)
    sub = lax.broadcasted_iota(jnp.int32, (8, n), 0)
    across = lambda x, k: jnp.broadcast_to(x[:, k : k + 1], (8, n))
    down = lambda x, s: jnp.broadcast_to(x[s : s + 1], (8, n))
    tiles = [[m[8 * t : 8 * t + 8] for t in range(n // 8)] for m in mats]
    for t in range(n // 8):
        base = 8 * t
        block = (lane >= base) & (lane < base + 8)
        for m in tiles:
            cols = [across(m[t], base + s) for s in range(8)]
            work = m[t]
            invs, rows, heads = [], [], []
            for s in range(8):
                here = lane == base + s
                below = sub > s
                inv = recip(down(cols[s], s))
                row = jnp.where(here, 1.0, down(work, s))
                mult = jnp.where(below, cols[s] * inv, 0.0)
                work = jnp.where(here & below, 0.0, work) - mult * row
                head = [down(cols[q], s) for q in range(s + 1, 8)]
                for q in range(s + 1, 8):
                    cols[q] = cols[q] - mult * head[q - s - 1]
                invs.append(inv)
                rows.append(jnp.where(block & (lane > base + s), 0.0, row))
                heads.append(head)
            m[t] = work
            for j in range(t + 1, n // 8):
                cols = [across(m[j], base + s) for s in range(8)]
                new = jnp.where(block, 0.0, m[j])
                for s in range(8):
                    mult = cols[s] * invs[s]
                    new = new - mult * rows[s]
                    for q in range(s + 1, 8):
                        cols[q] = cols[q] - mult * heads[s][q - s - 1]
                m[j] = new
    return [jnp.concatenate(m, 0) for m in tiles]


def positions(n):
    row = lax.broadcasted_iota(jnp.int32, (n, n), 0)
    col = lax.broadcasted_iota(jnp.int32, (n, n), 1)
    return row, col


def cholesky_pair(gram):
    (packed,) = eliminate([gram])
    row, col = positions(gram.shape[0])
    pivots = jnp.sum(jnp.where(row == col, packed, 0.0), 1, keepdims=True)
    scale = 1.0 / jnp.sqrt(pivots)
    upper = jnp.where(col >= row, packed, 0.0) * scale
    inverse = jnp.where(col < row, packed, jnp.where(col == row, 1.0, 0.0)) * scale
    return upper, inverse


def split(x):
    high = x.astype(jnp.bfloat16)
    return high, (x - high.astype(jnp.float32)).astype(jnp.bfloat16)


def dot_split(left, right, dims=NN):
    small = dot(left[1], right[0], dims, None) + dot(left[0], right[1], dims, None)
    return small + dot(left[0], right[0], dims, None)


def four_sum(refs):
    one, two, three, four = (ref[...] for ref in refs)
    return (one + two) + (three + four)


def panel_kernel(place_ref, *refs):
    stacks, (trailing_ref, panel_ref, mine_ref, away_ref, copy_ref, halves_ref, sems) = refs[:YS], refs[YS:]
    rows, cols = trailing_ref.shape
    chunk, width = stacks[0].shape[1:]
    tile = rows // PARTS
    copies = []
    for part in range(PARTS):
        span = pl.ds(part * tile, tile)
        copies.append(pltpu.make_async_copy(trailing_ref.at[span, :], copy_ref.at[span, :], sems.at[part]))
        copies[-1].start()
    y = place_ref[1] % YS
    for far, stack in enumerate(stacks):
        for z in range(ZS):
            at = (z * YS + (y ^ far)) * chunk
            panel_ref[pl.ds(pl.multiple_of(at, chunk), chunk), :] = stack[z]
    panel = panel_ref[...]
    gram = dot(panel, panel, TN)
    leading = jnp.where(place_ref[0] == 0, panel[:width], 0.0)
    total = jnp.zeros((width, cols), jnp.float32)
    for part in range(PARTS):
        copies[part].wait()
        span = slice(part * tile, (part + 1) * tile)
        total = total + dot(panel[span], copy_ref[span, :], TN)
    total = total.T
    for core in range(2):
        at = core * halves_ref.shape[0] // 2
        for block in (gram, total, leading):
            part = block.shape[0] // 2
            halves_ref[at : at + part, :] = block[core * part : (core + 1) * part]
            at += part
    core = place_ref[0] % 2
    half = halves_ref.shape[0] // 2
    mine_ref[...] = halves_ref[pl.ds(pl.multiple_of(core * half, 8), half), :]
    away_ref[...] = halves_ref[pl.ds(pl.multiple_of((1 - core) * half, 8), half), :]


def first_kernel(place_ref, mine_ref, other_ref, panel_ref, upper_ref, upper_copy_ref, inverse_ref, ortho_ref, gram_ref):
    part = panel_ref.shape[1] // 2
    mine, other = mine_ref[:part, :], other_ref[:part, :]
    first = place_ref[0] % 2 == 0
    gram = jnp.concatenate([jnp.where(first, mine, other), jnp.where(first, other, mine)], 0)
    upper, inverse = cholesky_pair(gram)
    upper_ref[...] = upper
    upper_copy_ref[...] = upper
    inverse_ref[...] = inverse
    ortho = dot(panel_ref[...], inverse, NT)
    ortho_ref[...] = ortho
    gram_ref[...] = dot(ortho, ortho, TN)


def second_kernel(*refs):
    upper_one_ref, inverse_one_ref, leading_ref = refs[4:7]
    inverse_two_ref, band_ref, band_inverse_t_ref, square_ref = refs[7:]
    upper, inverse = cholesky_pair(four_sum(refs[:4]))
    row, col = positions(upper.shape[0])
    inverse_one = inverse_one_ref[...]
    inverse_two_ref[...] = inverse
    band_ref[...] = dot(upper, upper_one_ref[...])
    band_inverse_t_ref[...] = dot(inverse, inverse_one)
    top = dot(dot(leading_ref[...], inverse_one, NT), inverse, NT)
    square_ref[...] = top + jnp.where(row == col, 1.0, 0.0)


def third_kernel(square_ref, factor_ref, upper_inverse_ref, square_inverse_ref):
    square = square_ref[...]
    one, two = eliminate([square, square.T])
    row, col = positions(square.shape[0])
    unit = jnp.where(row == col, 1.0, 0.0)
    pivots = jnp.sum(jnp.where(row == col, two, 0.0), 1, keepdims=True)
    upper = jnp.where(col >= row, one, 0.0)
    lower_inverse = jnp.where(col < row, one, unit)
    upper_inverse = (jnp.where(col < row, two, unit) / pivots).T
    factor_ref[...] = dot(upper, lower_inverse, NT)
    upper_inverse_ref[...] = upper_inverse
    square_inverse_ref[...] = dot(upper_inverse, lower_inverse)


def block_call(body, outs, name, cost, args, room=40, **more):
    return pl.pallas_call(
        body,
        out_shape=[jax.ShapeDtypeStruct(shape, jnp.float32) for shape in outs],
        name=name,
        cost_estimate=pl.CostEstimate(flops=cost, bytes_accessed=1 << 20, transcendentals=0),
        compiler_params=pltpu.CompilerParams(vmem_limit_bytes=room << 20),
        **more,
    )(*args)


def whole(count):
    return [pl.BlockSpec(memory_space=pltpu.VMEM)] * count


def scalars():
    return pl.BlockSpec(memory_space=pltpu.SMEM)


def unit_rows(start, count, width):
    place = start + lax.broadcasted_iota(jnp.int32, (count, width), 0)
    return jnp.where(place == lax.broadcasted_iota(jnp.int32, (count, width), 1), 1.0, 0.0)


def image_kernel(place_ref, *refs):
    products, edges = refs[:YS], refs[YS : YS + 2]
    ortho_ref, inverse_two_ref, band_inverse_t_ref, base_ref, image_ref, weight_ref = refs[YS + 2 :]
    cols, width = products[0].shape
    y = place_ref[1] % YS
    inverse_two = split(inverse_two_ref[...])
    band_inverse_t = band_inverse_t_ref[...]
    weight = jnp.zeros((width, width), jnp.float32)
    for far in range(YS):
        at = pl.multiple_of((y ^ far) * cols, cols)
        span = pl.ds(at, cols)
        start = place_ref[0] * (YS * cols) + at
        base = dot_split(split(ortho_ref[span, :]), inverse_two, NT) + unit_rows(start, cols, width)
        image = dot(products[far][...], band_inverse_t, NT) + edges[far // 2][(far % 2) * cols : (far % 2 + 1) * cols, :]
        base_ref[span, :] = base
        image_ref[span, :] = image
        weight = weight + dot_split(split(base), split(image), TN)
    weight_ref[...] = weight


def left_kernel(place_ref, base_ref, panel_ref, product_ref, edge_ref, inverse_one_ref, inverse_two_ref, band_inverse_t_ref, square_inverse_ref, upper_inverse_ref, left_ref, reflectors_ref, left_cols_ref, image_cols_ref):
    rows, width = base_ref.shape
    cols = panel_ref.shape[0]
    square_inverse = square_inverse_ref[...]
    table = split(jnp.concatenate([square_inverse, upper_inverse_ref[...]], 1))
    both = dot_split(split(base_ref[...]), table)
    left_ref[...] = both[:, :width]
    place = place_ref[0] * rows + lax.broadcasted_iota(jnp.int32, (rows, width), 0)
    lane = lax.broadcasted_iota(jnp.int32, (rows, width), 1)
    reflectors_ref[...] = jnp.where(place < lane, 0.0, jnp.where(place == lane, 1.0, both[:, width:]))
    ortho = dot(panel_ref[...], inverse_one_ref[...], NT)
    base = dot_split(split(ortho), split(inverse_two_ref[...]), NT) + unit_rows(place_ref[1] * cols, cols, width)
    left_cols_ref[...] = dot_split(split(base), split(square_inverse))
    image_cols_ref[...] = dot(product_ref[...], band_inverse_t_ref[...], NT) + edge_ref[...]


def update_kernel(*refs):
    trailing_ref, left_ref, image_ref, left_cols_ref, image_cols_ref, updated_ref, high_ref, low_ref, weight_high_ref, weight_low_ref = refs[4:]

    @pl.when(pl.program_id(0) == 0)
    def _():
        weight_high_ref[...], weight_low_ref[...] = split(0.5 * four_sum(refs[:4]))
        weight = weight_high_ref[...], weight_low_ref[...]
        left = left_cols_ref[...]
        right = image_cols_ref[...] - dot_split(split(left), weight)
        high_ref[...], low_ref[...] = split(jnp.concatenate([right, left], 1))

    left = left_ref[...]
    pieces = split(left)
    right = image_ref[...] - dot_split(pieces, (weight_high_ref[...], weight_low_ref[...]))
    rights = split(right)
    pair = tuple(jnp.concatenate([one, two], 1) for one, two in zip(pieces, rights))
    updated_ref[...] = trailing_ref[...] - dot_split(pair, (high_ref[...], low_ref[...]), NT)


def update(weights, trailing, left, image, left_cols, image_cols, steps=8):
    rows, cols = trailing.shape
    width = left.shape[1]
    tile = rows // steps
    moving = lambda step: (step, 0)
    fixed = lambda step: (0, 0)
    range_spec = pl.BlockSpec((tile, width), moving)
    cols_spec = pl.BlockSpec((cols, width), fixed)
    square_spec = pl.BlockSpec((width, width), fixed)
    tile_spec = pl.BlockSpec((tile, cols), moving)
    return block_call(
        update_kernel,
        [(rows, cols)],
        "update",
        1 << 32,
        [*weights, trailing, left, image, left_cols, image_cols],
        grid=(steps,),
        in_specs=[square_spec] * 4 + [tile_spec] + [range_spec] * 2 + [cols_spec] * 2,
        out_specs=[tile_spec],
        scratch_shapes=[pltpu.VMEM((cols, 2 * width), jnp.bfloat16)] * 2
        + [pltpu.VMEM((width, width), jnp.bfloat16)] * 2,
    )[0]


def swap_row(x, mask):
    return lax.ppermute(x, "prow", [(r, r ^ mask) for r in range(ROWS)])


def swap_y(x, mask):
    return lax.ppermute(x, "pcol", [(c, c ^ mask) for c in range(ZS * YS)])


def turn_z(x):
    pairs = [(r, z, z ^ (r // 2 + 4 * (r % 2))) for r in range(ROWS) for z in range(ZS)]
    return lax.ppermute(x, ("prow", "pcol"), [(place_of(r, z, y), place_of(r, t, y)) for r, z, t in pairs for y in range(YS)])


def turn_row(x, back=False):
    pairs = [(r, z, z ^ (r // 2 + 4 * (r % 2))) for r in range(ROWS) for z in range(ZS)]
    moves = [(place_of(r, z, y), place_of(t, z, y)) for r, z, t in pairs for y in range(YS)]
    if back:
        moves = [(t, f) for f, t in moves]
    return lax.ppermute(x, ("prow", "pcol"), moves)


def place_of(r, z, y):
    return (r * ZS + z) * YS + y


def three_rows(x):
    return [x] + [swap_row(x, 2 * mask) for mask in (1, 2, 3)]


def along_y(x):
    return [x] + [swap_y(x, mask) for mask in range(1, YS)]


def hold(*arrays):
    return lax.optimization_barrier(arrays)


def on_device(trailing, panel):
    rows, cols = trailing.shape
    chunk, width = panel.shape
    square = (width, width)
    row_index = lax.axis_index("prow")
    col_index = lax.axis_index("pcol")
    core = row_index % 2
    y = col_index % YS
    place = jnp.stack([row_index, col_index]).astype(jnp.int32)

    lines = [[z * YS + at for z in range(ZS)] for at in range(YS)]
    copies = jnp.broadcast_to(panel[None], (ZS, chunk, width))
    source, copies = hold(trailing[:width], copies)
    stack = lax.all_to_all(copies, "pcol", 0, 0, axis_index_groups=lines)
    edge = source.T
    pair = lax.ppermute(edge, "prow", [(0, 1)])
    pair = jnp.where(row_index == 0, edge, pair)
    arrived = [
        lax.ppermute(pair, "prow", [(0, 2 * far), (1, 2 * far + 1)]) for far in (1, 2, 3)
    ]
    edge_cols = jnp.where(row_index < 2, pair, arrived[0] + arrived[1] + arrived[2])

    edge_turned = turn_z(edge_cols)
    half = (cols + 2 * width) // 2
    panel_rows, mine, away = block_call(
        panel_kernel,
        [(rows, width), (half, width), (half, width)],
        "panel",
        1 << 32,
        [place] + along_y(stack) + [trailing],
        room=58,
        in_specs=[scalars()] + whole(YS) + [pl.BlockSpec(memory_space=pltpu.HBM)],
        out_specs=whole(3),
        scratch_shapes=[
            pltpu.VMEM((rows, cols), jnp.float32),
            pltpu.VMEM((2 * half, width), jnp.float32),
            pltpu.SemaphoreType.DMA((PARTS,)),
        ],
    )
    panel_rows, mine, away, edge_turned = hold(panel_rows, mine, away, edge_turned)

    edge_turned = turn_row(edge_turned)
    messages = three_rows(mine + swap_row(away, 1))
    messages[1], edge_turned, panel_cols = hold(
        messages[1], edge_turned, lax.dynamic_slice_in_dim(panel_rows, y * cols, cols, 0)
    )
    edge_pair = jnp.concatenate([edge_turned, swap_y(edge_turned, 1)], 0)
    panel_cols = turn_row(panel_cols, back=True)

    mine = (messages[0] + messages[1]) + (messages[2] + messages[3])
    mine, other = hold(mine, swap_row(mine, 1))
    summed = jnp.where(
        core == 0, jnp.stack([mine, other], 0), jnp.stack([other, mine], 0)
    )
    product_cols = summed[:, width // 2 : (width + cols) // 2].reshape(cols, width)
    leading = summed[:, (width + cols) // 2 :].reshape(square)
    product_turned = turn_z(product_cols)
    upper_one, upper_copy, inverse_one, ortho_rows, gram = block_call(
        first_kernel,
        [square, square, square, (rows, width), square],
        "first",
        1 << 33,
        [place, mine, other, panel_rows],
        in_specs=[scalars()] + whole(3),
        out_specs=whole(5),
    )
    gram, product_turned, panel_cols, edge_pair = hold(gram, product_turned, panel_cols, edge_pair)

    gram = gram + swap_row(gram, 1)
    product_turned = turn_row(product_turned)
    grams = three_rows(gram)
    *grams, product_turned = hold(*grams, product_turned)

    turned = along_y(product_turned)
    edges = [edge_pair, swap_y(edge_pair, 2)]
    inverse_two, band_block, band_inverse_t, top = block_call(
        second_kernel, [square] * 4, "second", 1 << 33, grams + [upper_copy, inverse_one, leading],
        in_specs=whole(7), out_specs=whole(4),
    )
    top, panel_cols = hold(top, panel_cols)
    panel_cols = turn_z(panel_cols)
    factor, upper_inverse, square_inverse = block_call(
        third_kernel, [square] * 3, "third", 1 << 33, [top], in_specs=whole(1), out_specs=whole(3)
    )
    square_inverse, *turned = hold(square_inverse, *turned)
    base, image, weight = block_call(
        image_kernel,
        [(rows, width)] * 2 + [square],
        "image",
        1 << 31,
        [place] + turned + edges + [ortho_rows, inverse_two, band_inverse_t],
        in_specs=[scalars()] + whole(YS + 5),
        out_specs=whole(3),
    )

    weight = weight + swap_row(weight, 1)
    weight, base = hold(weight, base)
    weights = three_rows(weight)
    left, reflectors, left_cols, image_cols = block_call(
        left_kernel,
        [(rows, width)] * 2 + [(cols, width)] * 2,
        "left",
        1 << 31,
        [place, base, panel_cols, product_cols, edge_cols, inverse_one, inverse_two, band_inverse_t, square_inverse, upper_inverse],
        in_specs=[scalars()] + whole(9),
        out_specs=whole(4),
    )
    updated = update(weights, trailing, left, image, left_cols, image_cols)
    return (updated, reflectors, factor, band_block, upper_one)


def solution(mesh):
    placed = (P("prow", "pcol"), P(("prow", "pcol"), None))
    return jax.shard_map(
        on_device,
        mesh=mesh,
        in_specs=placed,
        out_specs=(P("prow", "pcol"), P("prow", None), P(), P(), P()),
        check_vma=False,
    )
```

```python
import functools

import jax
import jax.numpy as jnp
from jax import lax
from jax.experimental import pallas as pl
from jax.experimental.pallas import tpu as pltpu
from jax.sharding import PartitionSpec as P

HIGHEST = lax.Precision.HIGHEST
ROWS, ZS, YS = 8, 8, 4
PARTS = 4
NN = (((1,), (0,)), ((), ()))
NT = (((1,), (1,)), ((), ()))
TN = (((0,), (0,)), ((), ()))


def dot(left, right, dims=NN, precision=HIGHEST):
    return lax.dot_general(
        left, right, dims, precision=precision, preferred_element_type=jnp.float32
    )


def eliminate(mats):
    n = mats[0].shape[0]
    lane = lax.broadcasted_iota(jnp.int32, (8, n), 1)
    sub = lax.broadcasted_iota(jnp.int32, (8, n), 0)
    across = lambda x, k: jnp.broadcast_to(x[:, k : k + 1], (8, n))
    down = lambda x, s: jnp.broadcast_to(x[s : s + 1], (8, n))
    tiles = [[m[8 * t : 8 * t + 8] for t in range(n // 8)] for m in mats]
    for t in range(n // 8):
        base = 8 * t
        block = (lane >= base) & (lane < base + 8)
        for m in tiles:
            cols = [across(m[t], base + s) for s in range(8)]
            work = m[t]
            invs, rows, heads = [], [], []
            for s in range(8):
                here = lane == base + s
                below = sub > s
                inv = pl.reciprocal(down(cols[s], s), approx=True)
                row = jnp.where(here, 1.0, down(work, s))
                low = jnp.where(below, cols[s], 0.0)
                work = jnp.where(here & below, 0.0, work) - (low * row) * inv
                head = [down(cols[q], s) for q in range(s + 1, 8)]
                for q in range(s + 1, 8):
                    cols[q] = cols[q] - (low * head[q - s - 1]) * inv
                invs.append(inv)
                rows.append(jnp.where(block & (lane > base + s), 0.0, row))
                heads.append(head)
            m[t] = work
            for j in range(t + 1, n // 8):
                cols = [across(m[j], base + s) for s in range(8)]
                new = jnp.where(block, 0.0, m[j])
                for s in range(8):
                    mult = cols[s] * invs[s]
                    new = new - mult * rows[s]
                    for q in range(s + 1, 8):
                        cols[q] = cols[q] - mult * heads[s][q - s - 1]
                m[j] = new
    return [jnp.concatenate(m, 0) for m in tiles]


def positions(n):
    row = lax.broadcasted_iota(jnp.int32, (n, n), 0)
    col = lax.broadcasted_iota(jnp.int32, (n, n), 1)
    return row, col


def cholesky_pair(gram):
    (packed,) = eliminate([gram])
    row, col = positions(gram.shape[0])
    pivots = jnp.sum(jnp.where(row == col, packed, 0.0), 1, keepdims=True)
    scale = 1.0 / jnp.sqrt(pivots)
    upper = jnp.where(col >= row, packed, 0.0) * scale
    inverse = jnp.where(col < row, packed, jnp.where(col == row, 1.0, 0.0)) * scale
    return upper, inverse


def split(x):
    high = x.astype(jnp.bfloat16)
    return high, (x - high.astype(jnp.float32)).astype(jnp.bfloat16)


def dot_split(left, right, dims=NN):
    small = dot(left[1], right[0], dims, None) + dot(left[0], right[1], dims, None)
    return small + dot(left[0], right[0], dims, None)


def four_sum(refs):
    one, two, three, four = (ref[...] for ref in refs)
    return (one + two) + (three + four)


def panel_kernel(place_ref, *refs):
    stacks, (trailing_ref, panel_ref, mine_ref, away_ref, halves_ref) = refs[:YS], refs[YS:]
    rows, cols = trailing_ref.shape
    chunk, width = stacks[0].shape[1:]
    tile = rows // PARTS
    y = place_ref[1] % YS
    for far, stack in enumerate(stacks):
        for z in range(ZS):
            at = (z * YS + (y ^ far)) * chunk
            panel_ref[pl.ds(pl.multiple_of(at, chunk), chunk), :] = stack[z]
    panel = panel_ref[...]
    gram = dot(panel, panel, TN)
    leading = jnp.where(place_ref[0] == 0, panel[:width], 0.0)
    total = jnp.zeros((width, cols), jnp.float32)
    for part in range(PARTS):
        span = slice(part * tile, (part + 1) * tile)
        total = total + dot(panel[span], trailing_ref[span, :], TN)
    total = total.T
    for core in range(2):
        at = core * halves_ref.shape[0] // 2
        for block in (gram, total, leading):
            part = block.shape[0] // 2
            halves_ref[at : at + part, :] = block[core * part : (core + 1) * part]
            at += part
    core = place_ref[0] % 2
    half = halves_ref.shape[0] // 2
    mine_ref[...] = halves_ref[pl.ds(pl.multiple_of(core * half, 8), half), :]
    away_ref[...] = halves_ref[pl.ds(pl.multiple_of((1 - core) * half, 8), half), :]


def first_kernel(place_ref, mine_ref, other_ref, panel_ref, upper_ref, upper_copy_ref, inverse_ref, ortho_ref, gram_ref):
    part = panel_ref.shape[1] // 2
    mine, other = mine_ref[:part, :], other_ref[:part, :]
    first = place_ref[0] % 2 == 0
    gram = jnp.concatenate([jnp.where(first, mine, other), jnp.where(first, other, mine)], 0)
    upper, inverse = cholesky_pair(gram)
    upper_ref[...] = upper
    upper_copy_ref[...] = upper
    inverse_ref[...] = inverse
    ortho = dot(panel_ref[...], inverse, NT)
    ortho_ref[...] = ortho
    gram_ref[...] = dot(ortho, ortho, TN)


def second_kernel(*refs):
    upper_one_ref, inverse_one_ref, leading_ref = refs[4:7]
    inverse_two_ref, band_ref, band_inverse_t_ref, square_ref = refs[7:]
    upper, inverse = cholesky_pair(four_sum(refs[:4]))
    row, col = positions(upper.shape[0])
    inverse_one = inverse_one_ref[...]
    inverse_two_ref[...] = inverse
    band_ref[...] = dot(upper, upper_one_ref[...])
    band_inverse_t_ref[...] = dot(inverse, inverse_one)
    top = dot(dot(leading_ref[...], inverse_one, NT), inverse, NT)
    square_ref[...] = top + jnp.where(row == col, 1.0, 0.0)


def third_kernel(square_ref, factor_ref, upper_inverse_ref, square_inverse_ref):
    square = square_ref[...]
    one, two = eliminate([square, square.T])
    row, col = positions(square.shape[0])
    unit = jnp.where(row == col, 1.0, 0.0)
    pivots = jnp.sum(jnp.where(row == col, two, 0.0), 1, keepdims=True)
    upper = jnp.where(col >= row, one, 0.0)
    lower_inverse = jnp.where(col < row, one, unit)
    upper_inverse = (jnp.where(col < row, two, unit) / pivots).T
    factor_ref[...] = dot(upper, lower_inverse, NT)
    upper_inverse_ref[...] = upper_inverse
    square_inverse_ref[...] = dot(upper_inverse, lower_inverse)


def block_call(body, outs, name, cost, args, **more):
    return pl.pallas_call(
        body,
        out_shape=[jax.ShapeDtypeStruct(shape, jnp.float32) for shape in outs],
        name=name,
        cost_estimate=pl.CostEstimate(flops=cost, bytes_accessed=1 << 20, transcendentals=0),
        compiler_params=pltpu.CompilerParams(vmem_limit_bytes=40 << 20),
        **more,
    )(*args)


def whole(count):
    return [pl.BlockSpec(memory_space=pltpu.VMEM)] * count


def scalars():
    return pl.BlockSpec(memory_space=pltpu.SMEM)


def unit_rows(start, count, width):
    place = start + lax.broadcasted_iota(jnp.int32, (count, width), 0)
    return jnp.where(place == lax.broadcasted_iota(jnp.int32, (count, width), 1), 1.0, 0.0)


def image_kernel(place_ref, *refs):
    products, edges = refs[:YS], refs[YS : YS + 2]
    ortho_ref, inverse_two_ref, band_inverse_t_ref, base_ref, image_ref, weight_ref = refs[YS + 2 :]
    cols, width = products[0].shape
    y = place_ref[1] % YS
    inverse_two = split(inverse_two_ref[...])
    band_inverse_t = band_inverse_t_ref[...]
    weight = jnp.zeros((width, width), jnp.float32)
    for far in range(YS):
        at = pl.multiple_of((y ^ far) * cols, cols)
        span = pl.ds(at, cols)
        start = place_ref[0] * (YS * cols) + at
        base = dot_split(split(ortho_ref[span, :]), inverse_two, NT) + unit_rows(start, cols, width)
        image = dot(products[far][...], band_inverse_t, NT) + edges[far // 2][(far % 2) * cols : (far % 2 + 1) * cols, :]
        base_ref[span, :] = base
        image_ref[span, :] = image
        weight = weight + dot_split(split(base), split(image), TN)
    weight_ref[...] = weight


def left_kernel(place_ref, base_ref, panel_ref, product_ref, edge_ref, inverse_one_ref, inverse_two_ref, band_inverse_t_ref, square_inverse_ref, upper_inverse_ref, left_ref, reflectors_ref, left_cols_ref, image_cols_ref):
    rows, width = base_ref.shape
    cols = panel_ref.shape[0]
    square_inverse = square_inverse_ref[...]
    table = split(jnp.concatenate([square_inverse, upper_inverse_ref[...]], 1))
    both = dot_split(split(base_ref[...]), table)
    left_ref[...] = both[:, :width]
    place = place_ref[0] * rows + lax.broadcasted_iota(jnp.int32, (rows, width), 0)
    lane = lax.broadcasted_iota(jnp.int32, (rows, width), 1)
    reflectors_ref[...] = jnp.where(place < lane, 0.0, jnp.where(place == lane, 1.0, both[:, width:]))
    ortho = dot(panel_ref[...], inverse_one_ref[...], NT)
    base = dot_split(split(ortho), split(inverse_two_ref[...]), NT) + unit_rows(place_ref[1] * cols, cols, width)
    left_cols_ref[...] = dot_split(split(base), split(square_inverse))
    image_cols_ref[...] = dot(product_ref[...], band_inverse_t_ref[...], NT) + edge_ref[...]


def update_kernel(*refs):
    trailing_ref, left_ref, image_ref, left_cols_ref, image_cols_ref, updated_ref, high_ref, low_ref, weight_high_ref, weight_low_ref = refs[4:]

    @pl.when(pl.program_id(0) == 0)
    def _():
        weight_high_ref[...], weight_low_ref[...] = split(0.5 * four_sum(refs[:4]))
        weight = weight_high_ref[...], weight_low_ref[...]
        left = left_cols_ref[...]
        right = image_cols_ref[...] - dot_split(split(left), weight)
        high_ref[...], low_ref[...] = split(jnp.concatenate([right, left], 1))

    left = left_ref[...]
    pieces = split(left)
    right = image_ref[...] - dot_split(pieces, (weight_high_ref[...], weight_low_ref[...]))
    rights = split(right)
    pair = tuple(jnp.concatenate([one, two], 1) for one, two in zip(pieces, rights))
    updated_ref[...] = trailing_ref[...] - dot_split(pair, (high_ref[...], low_ref[...]), NT)


def update(weights, trailing, left, image, left_cols, image_cols, steps=8):
    rows, cols = trailing.shape
    width = left.shape[1]
    tile = rows // steps
    moving = lambda step: (step, 0)
    fixed = lambda step: (0, 0)
    range_spec = pl.BlockSpec((tile, width), moving)
    cols_spec = pl.BlockSpec((cols, width), fixed)
    square_spec = pl.BlockSpec((width, width), fixed)
    tile_spec = pl.BlockSpec((tile, cols), moving)
    return block_call(
        update_kernel,
        [(rows, cols)],
        "update",
        1 << 32,
        [*weights, trailing, left, image, left_cols, image_cols],
        grid=(steps,),
        in_specs=[square_spec] * 4 + [tile_spec] + [range_spec] * 2 + [cols_spec] * 2,
        out_specs=[tile_spec],
        scratch_shapes=[pltpu.VMEM((cols, 2 * width), jnp.bfloat16)] * 2
        + [pltpu.VMEM((width, width), jnp.bfloat16)] * 2,
    )[0]


def swap_row(x, mask):
    return lax.ppermute(x, "prow", [(r, r ^ mask) for r in range(ROWS)])


def swap_y(x, mask):
    return lax.ppermute(x, "pcol", [(c, c ^ mask) for c in range(ZS * YS)])


def turn_z(x):
    pairs = [(r, z, z ^ (r // 2 + 4 * (r % 2))) for r in range(ROWS) for z in range(ZS)]
    return lax.ppermute(x, ("prow", "pcol"), [(place_of(r, z, y), place_of(r, t, y)) for r, z, t in pairs for y in range(YS)])


def turn_row(x, back=False):
    pairs = [(r, z, z ^ (r // 2 + 4 * (r % 2))) for r in range(ROWS) for z in range(ZS)]
    moves = [(place_of(r, z, y), place_of(t, z, y)) for r, z, t in pairs for y in range(YS)]
    if back:
        moves = [(t, f) for f, t in moves]
    return lax.ppermute(x, ("prow", "pcol"), moves)


def place_of(r, z, y):
    return (r * ZS + z) * YS + y


def three_rows(x):
    return [x] + [swap_row(x, 2 * mask) for mask in (1, 2, 3)]


def along_y(x):
    return [x] + [swap_y(x, mask) for mask in range(1, YS)]


def hold(*arrays):
    return lax.optimization_barrier(arrays)


def on_device(trailing, panel):
    rows, cols = trailing.shape
    chunk, width = panel.shape
    square = (width, width)
    row_index = lax.axis_index("prow")
    col_index = lax.axis_index("pcol")
    core = row_index % 2
    y = col_index % YS
    place = jnp.stack([row_index, col_index]).astype(jnp.int32)

    lines = [[z * YS + at for z in range(ZS)] for at in range(YS)]
    copies = jnp.broadcast_to(panel[None], (ZS, chunk, width))
    source, copies = hold(trailing[:width], copies)
    stack = lax.all_to_all(copies, "pcol", 0, 0, axis_index_groups=lines)
    edge = source.T
    pair = lax.ppermute(edge, "prow", [(0, 1)])
    pair = jnp.where(row_index == 0, edge, pair)
    arrived = [
        lax.ppermute(pair, "prow", [(0, 2 * far), (1, 2 * far + 1)]) for far in (1, 2, 3)
    ]
    edge_cols = jnp.where(row_index < 2, pair, arrived[0] + arrived[1] + arrived[2])

    edge_turned = turn_z(edge_cols)
    half = (cols + 2 * width) // 2
    panel_rows, mine, away = block_call(
        panel_kernel,
        [(rows, width), (half, width), (half, width)],
        "panel",
        1 << 32,
        [place] + along_y(stack) + [trailing],
        in_specs=[scalars()] + whole(YS + 1),
        out_specs=whole(3),
        scratch_shapes=[pltpu.VMEM((2 * half, width), jnp.float32)],
    )
    panel_rows, mine, away, edge_turned = hold(panel_rows, mine, away, edge_turned)

    edge_turned = turn_row(edge_turned)
    messages = three_rows(mine + swap_row(away, 1))
    panel_cols = lax.dynamic_slice_in_dim(panel_rows, y * cols, cols, 0)
    panel_cols = turn_row(panel_cols, back=True)
    messages[1], edge_turned, panel_cols = hold(messages[1], edge_turned, panel_cols)
    edge_pair = jnp.concatenate([edge_turned, swap_y(edge_turned, 1)], 0)
    panel_cols = turn_z(panel_cols)

    mine = (messages[0] + messages[1]) + (messages[2] + messages[3])
    mine, other = hold(mine, swap_row(mine, 1))
    summed = jnp.where(
        core == 0, jnp.stack([mine, other], 0), jnp.stack([other, mine], 0)
    )
    product_cols = summed[:, width // 2 : (width + cols) // 2].reshape(cols, width)
    leading = summed[:, (width + cols) // 2 :].reshape(square)
    product_turned = turn_z(product_cols)
    upper_one, upper_copy, inverse_one, ortho_rows, gram = block_call(
        first_kernel,
        [square, square, square, (rows, width), square],
        "first",
        1 << 33,
        [place, mine, other, panel_rows],
        in_specs=[scalars()] + whole(3),
        out_specs=whole(5),
    )
    gram, product_turned, panel_cols, edge_pair = hold(gram, product_turned, panel_cols, edge_pair)

    gram = gram + swap_row(gram, 1)
    product_turned = turn_row(product_turned)
    grams = three_rows(gram)
    *grams, product_turned = hold(*grams, product_turned)

    turned = along_y(product_turned)
    edges = [edge_pair, swap_y(edge_pair, 2)]
    inverse_two, band_block, band_inverse_t, top = block_call(
        second_kernel, [square] * 4, "second", 1 << 33, grams + [upper_copy, inverse_one, leading],
        in_specs=whole(7), out_specs=whole(4),
    )
    factor, upper_inverse, square_inverse = block_call(
        third_kernel, [square] * 3, "third", 1 << 33, [top], in_specs=whole(1), out_specs=whole(3)
    )
    square_inverse, *turned = hold(square_inverse, *turned)
    base, image, weight = block_call(
        image_kernel,
        [(rows, width)] * 2 + [square],
        "image",
        1 << 31,
        [place] + turned + edges + [ortho_rows, inverse_two, band_inverse_t],
        in_specs=[scalars()] + whole(YS + 5),
        out_specs=whole(3),
    )

    weight = weight + swap_row(weight, 1)
    weight, base = hold(weight, base)
    weights = three_rows(weight)
    left, reflectors, left_cols, image_cols = block_call(
        left_kernel,
        [(rows, width)] * 2 + [(cols, width)] * 2,
        "left",
        1 << 31,
        [place, base, panel_cols, product_cols, edge_cols, inverse_one, inverse_two, band_inverse_t, square_inverse, upper_inverse],
        in_specs=[scalars()] + whole(9),
        out_specs=whole(4),
    )
    updated = update(weights, trailing, left, image, left_cols, image_cols)
    return (updated, reflectors, factor, band_block, upper_one)


def solution(mesh):
    placed = (P("prow", "pcol"), P(("prow", "pcol"), None))
    return jax.shard_map(
        on_device,
        mesh=mesh,
        in_specs=placed,
        out_specs=(P("prow", "pcol"), P("prow", None), P(), P(), P()),
        check_vma=False,
    )
```

```python
import functools

import jax
import jax.numpy as jnp
from jax import lax
from jax.experimental import pallas as pl
from jax.experimental.pallas import tpu as pltpu
from jax.sharding import PartitionSpec as P

HIGHEST = lax.Precision.HIGHEST
ROWS, ZS, YS = 8, 8, 4
PARTS = 4
NN = (((1,), (0,)), ((), ()))
NT = (((1,), (1,)), ((), ()))
TN = (((0,), (0,)), ((), ()))


def dot(left, right, dims=NN, precision=HIGHEST):
    return lax.dot_general(
        left, right, dims, precision=precision, preferred_element_type=jnp.float32
    )


def eliminate(mats):
    n = mats[0].shape[0]
    lane = lax.broadcasted_iota(jnp.int32, (8, n), 1)
    sub = lax.broadcasted_iota(jnp.int32, (8, n), 0)
    across = lambda x, k: jnp.broadcast_to(x[:, k : k + 1], (8, n))
    down = lambda x, s: jnp.broadcast_to(x[s : s + 1], (8, n))
    tiles = [[m[8 * t : 8 * t + 8] for t in range(n // 8)] for m in mats]
    for t in range(n // 8):
        base = 8 * t
        block = (lane >= base) & (lane < base + 8)
        for m in tiles:
            cols = [across(m[t], base + s) for s in range(8)]
            work = m[t]
            invs, rows, heads = [], [], []
            for s in range(8):
                here = lane == base + s
                below = sub > s
                inv = pl.reciprocal(down(cols[s], s), approx=True)
                row = jnp.where(here, 1.0, down(work, s))
                low = jnp.where(below, cols[s], 0.0)
                work = jnp.where(here & below, 0.0, work) - (low * row) * inv
                head = [down(cols[q], s) for q in range(s + 1, 8)]
                for q in range(s + 1, 8):
                    cols[q] = cols[q] - (low * head[q - s - 1]) * inv
                invs.append(inv)
                rows.append(jnp.where(block & (lane > base + s), 0.0, row))
                heads.append(head)
            m[t] = work
            for j in range(t + 1, n // 8):
                cols = [across(m[j], base + s) for s in range(8)]
                new = jnp.where(block, 0.0, m[j])
                for s in range(8):
                    mult = cols[s] * invs[s]
                    new = new - mult * rows[s]
                    for q in range(s + 1, 8):
                        cols[q] = cols[q] - mult * heads[s][q - s - 1]
                m[j] = new
    return [jnp.concatenate(m, 0) for m in tiles]


def positions(n):
    row = lax.broadcasted_iota(jnp.int32, (n, n), 0)
    col = lax.broadcasted_iota(jnp.int32, (n, n), 1)
    return row, col


def cholesky_pair(gram):
    (packed,) = eliminate([gram])
    row, col = positions(gram.shape[0])
    pivots = jnp.sum(jnp.where(row == col, packed, 0.0), 1, keepdims=True)
    scale = 1.0 / jnp.sqrt(pivots)
    upper = jnp.where(col >= row, packed, 0.0) * scale
    inverse = jnp.where(col < row, packed, jnp.where(col == row, 1.0, 0.0)) * scale
    return upper, inverse


def split(x):
    high = x.astype(jnp.bfloat16)
    return high, (x - high.astype(jnp.float32)).astype(jnp.bfloat16)


def dot_split(left, right, dims=NN):
    small = dot(left[1], right[0], dims, None) + dot(left[0], right[1], dims, None)
    return small + dot(left[0], right[0], dims, None)


def four_sum(refs):
    one, two, three, four = (ref[...] for ref in refs)
    return (one + two) + (three + four)


def panel_kernel(place_ref, *refs):
    stacks, (trailing_ref, panel_ref, mine_ref, away_ref, halves_ref) = refs[:YS], refs[YS:]
    rows, cols = trailing_ref.shape
    chunk, width = stacks[0].shape[1:]
    tile = rows // PARTS
    y = place_ref[1] % YS
    for far, stack in enumerate(stacks):
        for z in range(ZS):
            at = (z * YS + (y ^ far)) * chunk
            panel_ref[pl.ds(pl.multiple_of(at, chunk), chunk), :] = stack[z]
    panel = panel_ref[...]
    gram = dot(panel, panel, TN)
    leading = jnp.where(place_ref[0] == 0, panel[:width], 0.0)
    total = jnp.zeros((width, cols), jnp.float32)
    for part in range(PARTS):
        span = slice(part * tile, (part + 1) * tile)
        total = total + dot(panel[span], trailing_ref[span, :], TN)
    total = total.T
    for core in range(2):
        at = core * halves_ref.shape[0] // 2
        for block in (gram, total, leading):
            part = block.shape[0] // 2
            halves_ref[at : at + part, :] = block[core * part : (core + 1) * part]
            at += part
    core = place_ref[0] % 2
    half = halves_ref.shape[0] // 2
    mine_ref[...] = halves_ref[pl.ds(pl.multiple_of(core * half, 8), half), :]
    away_ref[...] = halves_ref[pl.ds(pl.multiple_of((1 - core) * half, 8), half), :]


def first_kernel(place_ref, mine_ref, other_ref, panel_ref, upper_ref, upper_copy_ref, inverse_ref, ortho_ref, gram_ref):
    part = panel_ref.shape[1] // 2
    mine, other = mine_ref[:part, :], other_ref[:part, :]
    first = place_ref[0] % 2 == 0
    gram = jnp.concatenate([jnp.where(first, mine, other), jnp.where(first, other, mine)], 0)
    upper, inverse = cholesky_pair(gram)
    upper_ref[...] = upper
    upper_copy_ref[...] = upper
    inverse_ref[...] = inverse
    ortho = dot(panel_ref[...], inverse, NT)
    ortho_ref[...] = ortho
    gram_ref[...] = dot(ortho, ortho, TN)


def second_kernel(*refs):
    upper_one_ref, inverse_one_ref, leading_ref = refs[4:7]
    inverse_two_ref, band_ref, band_inverse_t_ref, square_ref = refs[7:]
    upper, inverse = cholesky_pair(four_sum(refs[:4]))
    row, col = positions(upper.shape[0])
    inverse_one = inverse_one_ref[...]
    inverse_two_ref[...] = inverse
    band_ref[...] = dot(upper, upper_one_ref[...])
    band_inverse_t_ref[...] = dot(inverse, inverse_one)
    top = dot(dot(leading_ref[...], inverse_one, NT), inverse, NT)
    square_ref[...] = top + jnp.where(row == col, 1.0, 0.0)


def third_kernel(square_ref, factor_ref, upper_inverse_ref, square_inverse_ref):
    square = square_ref[...]
    one, two = eliminate([square, square.T])
    row, col = positions(square.shape[0])
    unit = jnp.where(row == col, 1.0, 0.0)
    pivots = jnp.sum(jnp.where(row == col, two, 0.0), 1, keepdims=True)
    upper = jnp.where(col >= row, one, 0.0)
    lower_inverse = jnp.where(col < row, one, unit)
    upper_inverse = (jnp.where(col < row, two, unit) / pivots).T
    factor_ref[...] = dot(upper, lower_inverse, NT)
    upper_inverse_ref[...] = upper_inverse
    square_inverse_ref[...] = dot(upper_inverse, lower_inverse)


def block_call(body, outs, name, cost, args, **more):
    return pl.pallas_call(
        body,
        out_shape=[jax.ShapeDtypeStruct(shape, jnp.float32) for shape in outs],
        name=name,
        cost_estimate=pl.CostEstimate(flops=cost, bytes_accessed=1 << 20, transcendentals=0),
        compiler_params=pltpu.CompilerParams(vmem_limit_bytes=40 << 20),
        **more,
    )(*args)


def whole(count):
    return [pl.BlockSpec(memory_space=pltpu.VMEM)] * count


def scalars():
    return pl.BlockSpec(memory_space=pltpu.SMEM)


def unit_rows(start, count, width):
    place = start + lax.broadcasted_iota(jnp.int32, (count, width), 0)
    return jnp.where(place == lax.broadcasted_iota(jnp.int32, (count, width), 1), 1.0, 0.0)


def image_kernel(place_ref, *refs):
    products, edges = refs[:YS], refs[YS : 2 * YS]
    ortho_ref, inverse_two_ref, band_inverse_t_ref, base_ref, image_ref, weight_ref = refs[2 * YS :]
    cols, width = products[0].shape
    y = place_ref[1] % YS
    inverse_two = split(inverse_two_ref[...])
    band_inverse_t = band_inverse_t_ref[...]
    weight = jnp.zeros((width, width), jnp.float32)
    for far in range(YS):
        at = pl.multiple_of((y ^ far) * cols, cols)
        span = pl.ds(at, cols)
        start = place_ref[0] * (YS * cols) + at
        base = dot_split(split(ortho_ref[span, :]), inverse_two, NT) + unit_rows(start, cols, width)
        image = dot(products[far][...], band_inverse_t, NT) + edges[far][...]
        base_ref[span, :] = base
        image_ref[span, :] = image
        weight = weight + dot_split(split(base), split(image), TN)
    weight_ref[...] = weight


def left_kernel(place_ref, base_ref, panel_ref, product_ref, edge_ref, inverse_one_ref, inverse_two_ref, band_inverse_t_ref, square_inverse_ref, upper_inverse_ref, left_ref, reflectors_ref, left_cols_ref, image_cols_ref):
    rows, width = base_ref.shape
    cols = panel_ref.shape[0]
    square_inverse = square_inverse_ref[...]
    table = split(jnp.concatenate([square_inverse, upper_inverse_ref[...]], 1))
    both = dot_split(split(base_ref[...]), table)
    left_ref[...] = both[:, :width]
    place = place_ref[0] * rows + lax.broadcasted_iota(jnp.int32, (rows, width), 0)
    lane = lax.broadcasted_iota(jnp.int32, (rows, width), 1)
    reflectors_ref[...] = jnp.where(place < lane, 0.0, jnp.where(place == lane, 1.0, both[:, width:]))
    ortho = dot(panel_ref[...], inverse_one_ref[...], NT)
    base = dot_split(split(ortho), split(inverse_two_ref[...]), NT) + unit_rows(place_ref[1] * cols, cols, width)
    left_cols_ref[...] = dot_split(split(base), split(square_inverse))
    image_cols_ref[...] = dot(product_ref[...], band_inverse_t_ref[...], NT) + edge_ref[...]


def update_kernel(*refs):
    trailing_ref, left_ref, image_ref, left_cols_ref, image_cols_ref, updated_ref, high_ref, low_ref, weight_high_ref, weight_low_ref = refs[4:]

    @pl.when(pl.program_id(0) == 0)
    def _():
        weight_high_ref[...], weight_low_ref[...] = split(0.5 * four_sum(refs[:4]))
        weight = weight_high_ref[...], weight_low_ref[...]
        left = left_cols_ref[...]
        right = image_cols_ref[...] - dot_split(split(left), weight)
        high_ref[...], low_ref[...] = split(jnp.concatenate([right, left], 1))

    left = left_ref[...]
    pieces = split(left)
    right = image_ref[...] - dot_split(pieces, (weight_high_ref[...], weight_low_ref[...]))
    rights = split(right)
    pair = tuple(jnp.concatenate([one, two], 1) for one, two in zip(pieces, rights))
    updated_ref[...] = trailing_ref[...] - dot_split(pair, (high_ref[...], low_ref[...]), NT)


def update(weights, trailing, left, image, left_cols, image_cols, steps=8):
    rows, cols = trailing.shape
    width = left.shape[1]
    tile = rows // steps
    moving = lambda step: (step, 0)
    fixed = lambda step: (0, 0)
    range_spec = pl.BlockSpec((tile, width), moving)
    cols_spec = pl.BlockSpec((cols, width), fixed)
    square_spec = pl.BlockSpec((width, width), fixed)
    tile_spec = pl.BlockSpec((tile, cols), moving)
    return block_call(
        update_kernel,
        [(rows, cols)],
        "update",
        1 << 32,
        [*weights, trailing, left, image, left_cols, image_cols],
        grid=(steps,),
        in_specs=[square_spec] * 4 + [tile_spec] + [range_spec] * 2 + [cols_spec] * 2,
        out_specs=[tile_spec],
        scratch_shapes=[pltpu.VMEM((cols, 2 * width), jnp.bfloat16)] * 2
        + [pltpu.VMEM((width, width), jnp.bfloat16)] * 2,
    )[0]


def swap_row(x, mask):
    return lax.ppermute(x, "prow", [(r, r ^ mask) for r in range(ROWS)])


def swap_y(x, mask):
    return lax.ppermute(x, "pcol", [(c, c ^ mask) for c in range(ZS * YS)])


def turn_z(x):
    pairs = [(r, z, z ^ (r // 2 + 4 * (r % 2))) for r in range(ROWS) for z in range(ZS)]
    return lax.ppermute(x, ("prow", "pcol"), [(place_of(r, z, y), place_of(r, t, y)) for r, z, t in pairs for y in range(YS)])


def turn_row(x, back=False):
    pairs = [(r, z, z ^ (r // 2 + 4 * (r % 2))) for r in range(ROWS) for z in range(ZS)]
    moves = [(place_of(r, z, y), place_of(t, z, y)) for r, z, t in pairs for y in range(YS)]
    if back:
        moves = [(t, f) for f, t in moves]
    return lax.ppermute(x, ("prow", "pcol"), moves)


def place_of(r, z, y):
    return (r * ZS + z) * YS + y


def three_rows(x):
    return [x] + [swap_row(x, 2 * mask) for mask in (1, 2, 3)]


def along_y(x):
    return [x] + [swap_y(x, mask) for mask in range(1, YS)]


def hold(*arrays):
    return lax.optimization_barrier(arrays)


def on_device(trailing, panel):
    rows, cols = trailing.shape
    chunk, width = panel.shape
    square = (width, width)
    row_index = lax.axis_index("prow")
    col_index = lax.axis_index("pcol")
    core = row_index % 2
    y = col_index % YS
    place = jnp.stack([row_index, col_index]).astype(jnp.int32)

    lines = [[z * YS + at for z in range(ZS)] for at in range(YS)]
    copies = jnp.broadcast_to(panel[None], (ZS, chunk, width))
    source, copies = hold(trailing[:width], copies)
    stack = lax.all_to_all(copies, "pcol", 0, 0, axis_index_groups=lines)
    edge = source.T
    pair = lax.ppermute(edge, "prow", [(0, 1)])
    pair = jnp.where(row_index == 0, edge, pair)
    arrived = [
        lax.ppermute(pair, "prow", [(0, 2 * far), (1, 2 * far + 1)]) for far in (1, 2, 3)
    ]
    edge_cols = jnp.where(row_index < 2, pair, arrived[0] + arrived[1] + arrived[2])

    edge_turned = turn_z(edge_cols)
    half = (cols + 2 * width) // 2
    panel_rows, mine, away = block_call(
        panel_kernel,
        [(rows, width), (half, width), (half, width)],
        "panel",
        1 << 32,
        [place] + along_y(stack) + [trailing],
        in_specs=[scalars()] + whole(YS + 1),
        out_specs=whole(3),
        scratch_shapes=[pltpu.VMEM((2 * half, width), jnp.float32)],
    )
    panel_rows, mine, away, edge_turned = hold(panel_rows, mine, away, edge_turned)

    edge_turned = turn_row(edge_turned)
    messages = three_rows(mine + swap_row(away, 1))
    panel_cols = lax.dynamic_slice_in_dim(panel_rows, y * cols, cols, 0)
    panel_cols = turn_row(panel_cols, back=True)
    messages[1], edge_turned, panel_cols = hold(messages[1], edge_turned, panel_cols)
    edges = along_y(edge_turned)

    mine = (messages[0] + messages[1]) + (messages[2] + messages[3])
    mine, other = hold(mine, swap_row(mine, 1))
    summed = jnp.where(
        core == 0, jnp.stack([mine, other], 0), jnp.stack([other, mine], 0)
    )
    product_cols = summed[:, width // 2 : (width + cols) // 2].reshape(cols, width)
    leading = summed[:, (width + cols) // 2 :].reshape(square)
    product_turned = turn_z(product_cols)
    upper_one, upper_copy, inverse_one, ortho_rows, gram = block_call(
        first_kernel,
        [square, square, square, (rows, width), square],
        "first",
        1 << 33,
        [place, mine, other, panel_rows],
        in_specs=[scalars()] + whole(3),
        out_specs=whole(5),
    )
    gram, product_turned, *edges = hold(gram, product_turned, *edges)

    gram, product_turned = hold(gram + swap_row(gram, 1), product_turned)
    product_turned = turn_row(product_turned)
    panel_cols = turn_z(panel_cols)
    grams = three_rows(gram)
    *grams, product_turned, panel_cols = hold(*grams, product_turned, panel_cols)

    turned = along_y(product_turned)
    inverse_two, band_block, band_inverse_t, top = block_call(
        second_kernel, [square] * 4, "second", 1 << 33, grams + [upper_copy, inverse_one, leading],
        in_specs=whole(7), out_specs=whole(4),
    )
    factor, upper_inverse, square_inverse = block_call(
        third_kernel, [square] * 3, "third", 1 << 33, [top], in_specs=whole(1), out_specs=whole(3)
    )
    square_inverse, *turned = hold(square_inverse, *turned)
    base, image, weight = block_call(
        image_kernel,
        [(rows, width)] * 2 + [square],
        "image",
        1 << 31,
        [place] + turned + edges + [ortho_rows, inverse_two, band_inverse_t],
        in_specs=[scalars()] + whole(2 * YS + 3),
        out_specs=whole(3),
    )

    weight = weight + swap_row(weight, 1)
    weight, base = hold(weight, base)
    weights = three_rows(weight)
    left, reflectors, left_cols, image_cols = block_call(
        left_kernel,
        [(rows, width)] * 2 + [(cols, width)] * 2,
        "left",
        1 << 31,
        [place, base, panel_cols, product_cols, edge_cols, inverse_one, inverse_two, band_inverse_t, square_inverse, upper_inverse],
        in_specs=[scalars()] + whole(9),
        out_specs=whole(4),
    )
    updated = update(weights, trailing, left, image, left_cols, image_cols)
    return (updated, reflectors, factor, band_block, upper_one)


def solution(mesh):
    placed = (P("prow", "pcol"), P(("prow", "pcol"), None))
    return jax.shard_map(
        on_device,
        mesh=mesh,
        in_specs=placed,
        out_specs=(P("prow", "pcol"), P("prow", None), P(), P(), P()),
        check_vma=False,
    )
```

```python
import functools

import jax
import jax.numpy as jnp
from jax import lax
from jax.experimental import pallas as pl
from jax.experimental.pallas import tpu as pltpu
from jax.sharding import PartitionSpec as P

HIGHEST = lax.Precision.HIGHEST
ROWS, ZS, YS = 8, 8, 4
PARTS = 4
NN = (((1,), (0,)), ((), ()))
NT = (((1,), (1,)), ((), ()))
TN = (((0,), (0,)), ((), ()))


def dot(left, right, dims=NN, precision=HIGHEST):
    return lax.dot_general(
        left, right, dims, precision=precision, preferred_element_type=jnp.float32
    )


def eliminate(mats):
    n = mats[0].shape[0]
    lane = lax.broadcasted_iota(jnp.int32, (8, n), 1)
    sub = lax.broadcasted_iota(jnp.int32, (8, n), 0)
    across = lambda x, k: jnp.broadcast_to(x[:, k : k + 1], (8, n))
    down = lambda x, s: jnp.broadcast_to(x[s : s + 1], (8, n))
    tiles = [[m[8 * t : 8 * t + 8] for t in range(n // 8)] for m in mats]
    for t in range(n // 8):
        base = 8 * t
        block = (lane >= base) & (lane < base + 8)
        for m in tiles:
            cols = [across(m[t], base + s) for s in range(8)]
            work = m[t]
            invs, rows, heads = [], [], []
            for s in range(8):
                here = lane == base + s
                below = sub > s
                inv = pl.reciprocal(down(cols[s], s), approx=True)
                row = jnp.where(here, 1.0, down(work, s))
                low = jnp.where(below, cols[s], 0.0)
                work = jnp.where(here & below, 0.0, work) - (low * row) * inv
                head = [down(cols[q], s) for q in range(s + 1, 8)]
                for q in range(s + 1, 8):
                    cols[q] = cols[q] - (low * head[q - s - 1]) * inv
                invs.append(inv)
                rows.append(jnp.where(block & (lane > base + s), 0.0, row))
                heads.append(head)
            m[t] = work
            for j in range(t + 1, n // 8):
                cols = [across(m[j], base + s) for s in range(8)]
                new = jnp.where(block, 0.0, m[j])
                for s in range(8):
                    mult = cols[s] * invs[s]
                    new = new - mult * rows[s]
                    for q in range(s + 1, 8):
                        cols[q] = cols[q] - mult * heads[s][q - s - 1]
                m[j] = new
    return [jnp.concatenate(m, 0) for m in tiles]


def positions(n):
    row = lax.broadcasted_iota(jnp.int32, (n, n), 0)
    col = lax.broadcasted_iota(jnp.int32, (n, n), 1)
    return row, col


def cholesky_pair(gram):
    (packed,) = eliminate([gram])
    row, col = positions(gram.shape[0])
    pivots = jnp.sum(jnp.where(row == col, packed, 0.0), 1, keepdims=True)
    scale = 1.0 / jnp.sqrt(pivots)
    upper = jnp.where(col >= row, packed, 0.0) * scale
    inverse = jnp.where(col < row, packed, jnp.where(col == row, 1.0, 0.0)) * scale
    return upper, inverse


def split(x):
    high = x.astype(jnp.bfloat16)
    return high, (x - high.astype(jnp.float32)).astype(jnp.bfloat16)


def dot_split(left, right, dims=NN):
    small = dot(left[1], right[0], dims, None) + dot(left[0], right[1], dims, None)
    return small + dot(left[0], right[0], dims, None)


def four_sum(refs):
    one, two, three, four = (ref[...] for ref in refs)
    return (one + two) + (three + four)


def panel_kernel(place_ref, *refs):
    stacks, (trailing_ref, panel_ref, mine_ref, away_ref, halves_ref) = refs[:YS], refs[YS:]
    rows, cols = trailing_ref.shape
    chunk, width = stacks[0].shape[1:]
    tile = rows // PARTS
    y = place_ref[1] % YS
    for far, stack in enumerate(stacks):
        for z in range(ZS):
            at = (z * YS + (y ^ far)) * chunk
            panel_ref[pl.ds(pl.multiple_of(at, chunk), chunk), :] = stack[z]
    panel = panel_ref[...]
    gram = dot(panel, panel, TN)
    leading = jnp.where(place_ref[0] == 0, panel[:width], 0.0)
    total = jnp.zeros((width, cols), jnp.float32)
    for part in range(PARTS):
        span = slice(part * tile, (part + 1) * tile)
        total = total + dot(panel[span], trailing_ref[span, :], TN)
    total = total.T
    for core in range(2):
        at = core * halves_ref.shape[0] // 2
        for block in (gram, total, leading):
            part = block.shape[0] // 2
            halves_ref[at : at + part, :] = block[core * part : (core + 1) * part]
            at += part
    core = place_ref[0] % 2
    half = halves_ref.shape[0] // 2
    mine_ref[...] = halves_ref[pl.ds(pl.multiple_of(core * half, 8), half), :]
    away_ref[...] = halves_ref[pl.ds(pl.multiple_of((1 - core) * half, 8), half), :]


def first_kernel(place_ref, mine_ref, other_ref, panel_ref, upper_ref, upper_copy_ref, inverse_ref, ortho_ref, gram_ref):
    part = panel_ref.shape[1] // 2
    mine, other = mine_ref[:part, :], other_ref[:part, :]
    first = place_ref[0] % 2 == 0
    gram = jnp.concatenate([jnp.where(first, mine, other), jnp.where(first, other, mine)], 0)
    upper, inverse = cholesky_pair(gram)
    upper_ref[...] = upper
    upper_copy_ref[...] = upper
    inverse_ref[...] = inverse
    ortho = dot(panel_ref[...], inverse, NT)
    ortho_ref[...] = ortho
    gram_ref[...] = dot(ortho, ortho, TN)


def second_kernel(*refs):
    upper_one_ref, inverse_one_ref, leading_ref = refs[4:7]
    inverse_two_ref, band_ref, band_inverse_t_ref, square_ref = refs[7:]
    upper, inverse = cholesky_pair(four_sum(refs[:4]))
    row, col = positions(upper.shape[0])
    inverse_one = inverse_one_ref[...]
    inverse_two_ref[...] = inverse
    band_ref[...] = dot(upper, upper_one_ref[...])
    band_inverse_t_ref[...] = dot(inverse, inverse_one)
    top = dot(dot(leading_ref[...], inverse_one, NT), inverse, NT)
    square_ref[...] = top + jnp.where(row == col, 1.0, 0.0)


def third_kernel(square_ref, factor_ref, upper_inverse_ref, square_inverse_ref):
    square = square_ref[...]
    one, two = eliminate([square, square.T])
    row, col = positions(square.shape[0])
    unit = jnp.where(row == col, 1.0, 0.0)
    pivots = jnp.sum(jnp.where(row == col, two, 0.0), 1, keepdims=True)
    upper = jnp.where(col >= row, one, 0.0)
    lower_inverse = jnp.where(col < row, one, unit)
    upper_inverse = (jnp.where(col < row, two, unit) / pivots).T
    factor_ref[...] = dot(upper, lower_inverse, NT)
    upper_inverse_ref[...] = upper_inverse
    square_inverse_ref[...] = dot(upper_inverse, lower_inverse)


def block_call(body, outs, name, cost, args, **more):
    return pl.pallas_call(
        body,
        out_shape=[jax.ShapeDtypeStruct(shape, jnp.float32) for shape in outs],
        name=name,
        cost_estimate=pl.CostEstimate(flops=cost, bytes_accessed=1 << 20, transcendentals=0),
        compiler_params=pltpu.CompilerParams(vmem_limit_bytes=40 << 20),
        **more,
    )(*args)


def whole(count):
    return [pl.BlockSpec(memory_space=pltpu.VMEM)] * count


def scalars():
    return pl.BlockSpec(memory_space=pltpu.SMEM)


def unit_rows(start, count, width):
    place = start + lax.broadcasted_iota(jnp.int32, (count, width), 0)
    return jnp.where(place == lax.broadcasted_iota(jnp.int32, (count, width), 1), 1.0, 0.0)


def image_kernel(place_ref, *refs):
    products, edges = refs[:YS], refs[YS : 2 * YS]
    ortho_ref, inverse_two_ref, band_inverse_t_ref, base_ref, image_ref, weight_ref = refs[2 * YS :]
    cols, width = products[0].shape
    y = place_ref[1] % YS
    inverse_two = split(inverse_two_ref[...])
    band_inverse_t = band_inverse_t_ref[...]
    weight = jnp.zeros((width, width), jnp.float32)
    for far in range(YS):
        at = pl.multiple_of((y ^ far) * cols, cols)
        span = pl.ds(at, cols)
        start = place_ref[0] * (YS * cols) + at
        base = dot_split(split(ortho_ref[span, :]), inverse_two, NT) + unit_rows(start, cols, width)
        image = dot(products[far][...], band_inverse_t, NT) + edges[far][...]
        base_ref[span, :] = base
        image_ref[span, :] = image
        weight = weight + dot_split(split(base), split(image), TN)
    weight_ref[...] = weight


def left_kernel(place_ref, base_ref, panel_ref, product_ref, edge_ref, inverse_one_ref, inverse_two_ref, band_inverse_t_ref, square_inverse_ref, upper_inverse_ref, left_ref, reflectors_ref, left_cols_ref, image_cols_ref):
    rows, width = base_ref.shape
    cols = panel_ref.shape[0]
    square_inverse = square_inverse_ref[...]
    table = split(jnp.concatenate([square_inverse, upper_inverse_ref[...]], 1))
    both = dot_split(split(base_ref[...]), table)
    left_ref[...] = both[:, :width]
    place = place_ref[0] * rows + lax.broadcasted_iota(jnp.int32, (rows, width), 0)
    lane = lax.broadcasted_iota(jnp.int32, (rows, width), 1)
    reflectors_ref[...] = jnp.where(place < lane, 0.0, jnp.where(place == lane, 1.0, both[:, width:]))
    ortho = dot(panel_ref[...], inverse_one_ref[...], NT)
    base = dot_split(split(ortho), split(inverse_two_ref[...]), NT) + unit_rows(place_ref[1] * cols, cols, width)
    left_cols_ref[...] = dot_split(split(base), split(square_inverse))
    image_cols_ref[...] = dot(product_ref[...], band_inverse_t_ref[...], NT) + edge_ref[...]


def update_kernel(*refs):
    trailing_ref, left_ref, image_ref, left_cols_ref, image_cols_ref, updated_ref, high_ref, low_ref, weight_high_ref, weight_low_ref = refs[4:]

    @pl.when(pl.program_id(0) == 0)
    def _():
        weight_high_ref[...], weight_low_ref[...] = split(0.5 * four_sum(refs[:4]))
        weight = weight_high_ref[...], weight_low_ref[...]
        left = left_cols_ref[...]
        right = image_cols_ref[...] - dot_split(split(left), weight)
        high_ref[...], low_ref[...] = split(jnp.concatenate([right, left], 1))

    left = left_ref[...]
    pieces = split(left)
    right = image_ref[...] - dot_split(pieces, (weight_high_ref[...], weight_low_ref[...]))
    rights = split(right)
    pair = tuple(jnp.concatenate([one, two], 1) for one, two in zip(pieces, rights))
    updated_ref[...] = trailing_ref[...] - dot_split(pair, (high_ref[...], low_ref[...]), NT)


def update(weights, trailing, left, image, left_cols, image_cols, steps=8):
    rows, cols = trailing.shape
    width = left.shape[1]
    tile = rows // steps
    moving = lambda step: (step, 0)
    fixed = lambda step: (0, 0)
    range_spec = pl.BlockSpec((tile, width), moving)
    cols_spec = pl.BlockSpec((cols, width), fixed)
    square_spec = pl.BlockSpec((width, width), fixed)
    tile_spec = pl.BlockSpec((tile, cols), moving)
    return block_call(
        update_kernel,
        [(rows, cols)],
        "update",
        1 << 32,
        [*weights, trailing, left, image, left_cols, image_cols],
        grid=(steps,),
        in_specs=[square_spec] * 4 + [tile_spec] + [range_spec] * 2 + [cols_spec] * 2,
        out_specs=[tile_spec],
        scratch_shapes=[pltpu.VMEM((cols, 2 * width), jnp.bfloat16)] * 2
        + [pltpu.VMEM((width, width), jnp.bfloat16)] * 2,
    )[0]


def swap_row(x, mask):
    return lax.ppermute(x, "prow", [(r, r ^ mask) for r in range(ROWS)])


def swap_y(x, mask):
    return lax.ppermute(x, "pcol", [(c, c ^ mask) for c in range(ZS * YS)])


def turn_z(x):
    pairs = [(r, z, z ^ (r // 2 + 4 * (r % 2))) for r in range(ROWS) for z in range(ZS)]
    return lax.ppermute(x, ("prow", "pcol"), [(place_of(r, z, y), place_of(r, t, y)) for r, z, t in pairs for y in range(YS)])


def turn_row(x, back=False):
    pairs = [(r, z, z ^ (r // 2 + 4 * (r % 2))) for r in range(ROWS) for z in range(ZS)]
    moves = [(place_of(r, z, y), place_of(t, z, y)) for r, z, t in pairs for y in range(YS)]
    if back:
        moves = [(t, f) for f, t in moves]
    return lax.ppermute(x, ("prow", "pcol"), moves)


def place_of(r, z, y):
    return (r * ZS + z) * YS + y


def three_rows(x):
    return [x] + [swap_row(x, 2 * mask) for mask in (1, 2, 3)]


def along_y(x):
    return [x] + [swap_y(x, mask) for mask in range(1, YS)]


def hold(*arrays):
    return lax.optimization_barrier(arrays)


def on_device(trailing, panel):
    rows, cols = trailing.shape
    chunk, width = panel.shape
    square = (width, width)
    row_index = lax.axis_index("prow")
    col_index = lax.axis_index("pcol")
    core = row_index % 2
    y = col_index % YS
    place = jnp.stack([row_index, col_index]).astype(jnp.int32)

    lines = [[z * YS + at for z in range(ZS)] for at in range(YS)]
    copies = jnp.broadcast_to(panel[None], (ZS, chunk, width))
    source, copies = hold(trailing[:width], copies)
    stack = lax.all_to_all(copies, "pcol", 0, 0, axis_index_groups=lines)
    edge = source.T
    pair = lax.ppermute(edge, "prow", [(0, 1)])
    pair = jnp.where(row_index == 0, edge, pair)
    arrived = [
        lax.ppermute(pair, "prow", [(0, 2 * far), (1, 2 * far + 1)]) for far in (1, 2, 3)
    ]
    edge_cols = jnp.where(row_index < 2, pair, arrived[0] + arrived[1] + arrived[2])

    edge_turned = turn_z(edge_cols)
    half = (cols + 2 * width) // 2
    panel_rows, mine, away = block_call(
        panel_kernel,
        [(rows, width), (half, width), (half, width)],
        "panel",
        1 << 32,
        [place] + along_y(stack) + [trailing],
        in_specs=[scalars()] + whole(YS + 1),
        out_specs=whole(3),
        scratch_shapes=[pltpu.VMEM((2 * half, width), jnp.float32)],
    )
    panel_rows, mine, away, edge_turned = hold(panel_rows, mine, away, edge_turned)

    edge_turned = turn_row(edge_turned)
    messages = three_rows(mine + swap_row(away, 1))
    panel_cols = lax.dynamic_slice_in_dim(panel_rows, y * cols, cols, 0)
    messages[1], edge_turned, panel_cols = hold(messages[1], edge_turned, panel_cols)
    edges = along_y(edge_turned)
    panel_cols = turn_row(panel_cols, back=True)

    mine = (messages[0] + messages[1]) + (messages[2] + messages[3])
    mine, other = hold(mine, swap_row(mine, 1))
    summed = jnp.where(
        core == 0, jnp.stack([mine, other], 0), jnp.stack([other, mine], 0)
    )
    product_cols = summed[:, width // 2 : (width + cols) // 2].reshape(cols, width)
    leading = summed[:, (width + cols) // 2 :].reshape(square)
    product_turned = turn_z(product_cols)
    upper_one, upper_copy, inverse_one, ortho_rows, gram = block_call(
        first_kernel,
        [square, square, square, (rows, width), square],
        "first",
        1 << 33,
        [place, mine, other, panel_rows],
        in_specs=[scalars()] + whole(3),
        out_specs=whole(5),
    )
    gram, product_turned, panel_cols, *edges = hold(gram, product_turned, panel_cols, *edges)

    gram, product_turned = hold(gram + swap_row(gram, 1), product_turned)
    product_turned = turn_row(product_turned)
    panel_cols = turn_z(panel_cols)
    grams = three_rows(gram)
    *grams, product_turned, panel_cols = hold(*grams, product_turned, panel_cols)

    turned = along_y(product_turned)
    inverse_two, band_block, band_inverse_t, top = block_call(
        second_kernel, [square] * 4, "second", 1 << 33, grams + [upper_copy, inverse_one, leading],
        in_specs=whole(7), out_specs=whole(4),
    )
    factor, upper_inverse, square_inverse = block_call(
        third_kernel, [square] * 3, "third", 1 << 33, [top], in_specs=whole(1), out_specs=whole(3)
    )
    square_inverse, *turned = hold(square_inverse, *turned)
    base, image, weight = block_call(
        image_kernel,
        [(rows, width)] * 2 + [square],
        "image",
        1 << 31,
        [place] + turned + edges + [ortho_rows, inverse_two, band_inverse_t],
        in_specs=[scalars()] + whole(2 * YS + 3),
        out_specs=whole(3),
    )

    weight = weight + swap_row(weight, 1)
    weight, base = hold(weight, base)
    weights = three_rows(weight)
    left, reflectors, left_cols, image_cols = block_call(
        left_kernel,
        [(rows, width)] * 2 + [(cols, width)] * 2,
        "left",
        1 << 31,
        [place, base, panel_cols, product_cols, edge_cols, inverse_one, inverse_two, band_inverse_t, square_inverse, upper_inverse],
        in_specs=[scalars()] + whole(9),
        out_specs=whole(4),
    )
    updated = update(weights, trailing, left, image, left_cols, image_cols)
    return (updated, reflectors, factor, band_block, upper_one)


def solution(mesh):
    placed = (P("prow", "pcol"), P(("prow", "pcol"), None))
    return jax.shard_map(
        on_device,
        mesh=mesh,
        in_specs=placed,
        out_specs=(P("prow", "pcol"), P("prow", None), P(), P(), P()),
        check_vma=False,
    )
```

```python
import functools

import jax
import jax.numpy as jnp
from jax import lax
from jax.experimental import pallas as pl
from jax.experimental.pallas import tpu as pltpu
from jax.sharding import PartitionSpec as P

HIGHEST = lax.Precision.HIGHEST
ROWS, ZS, YS = 8, 8, 4
PARTS = 4
NN = (((1,), (0,)), ((), ()))
NT = (((1,), (1,)), ((), ()))
TN = (((0,), (0,)), ((), ()))


def dot(left, right, dims=NN, precision=HIGHEST):
    return lax.dot_general(
        left, right, dims, precision=precision, preferred_element_type=jnp.float32
    )


def eliminate(mats):
    n = mats[0].shape[0]
    lane = lax.broadcasted_iota(jnp.int32, (8, n), 1)
    sub = lax.broadcasted_iota(jnp.int32, (8, n), 0)
    across = lambda x, k: jnp.broadcast_to(x[:, k : k + 1], (8, n))
    down = lambda x, s: jnp.broadcast_to(x[s : s + 1], (8, n))
    tiles = [[m[8 * t : 8 * t + 8] for t in range(n // 8)] for m in mats]
    for t in range(n // 8):
        base = 8 * t
        block = (lane >= base) & (lane < base + 8)
        for m in tiles:
            cols = [across(m[t], base + s) for s in range(8)]
            work = m[t]
            invs, rows, heads = [], [], []
            for s in range(8):
                here = lane == base + s
                below = sub > s
                inv = pl.reciprocal(down(cols[s], s), approx=True)
                row = jnp.where(here, 1.0, down(work, s))
                low = jnp.where(below, cols[s], 0.0)
                work = jnp.where(here & below, 0.0, work) - (low * row) * inv
                head = [down(cols[q], s) for q in range(s + 1, 8)]
                for q in range(s + 1, 8):
                    cols[q] = cols[q] - (low * head[q - s - 1]) * inv
                invs.append(inv)
                rows.append(jnp.where(block & (lane > base + s), 0.0, row))
                heads.append(head)
            m[t] = work
            for j in range(t + 1, n // 8):
                cols = [across(m[j], base + s) for s in range(8)]
                new = jnp.where(block, 0.0, m[j])
                for s in range(8):
                    mult = cols[s] * invs[s]
                    new = new - mult * rows[s]
                    for q in range(s + 1, 8):
                        cols[q] = cols[q] - mult * heads[s][q - s - 1]
                m[j] = new
    return [jnp.concatenate(m, 0) for m in tiles]


def positions(n):
    row = lax.broadcasted_iota(jnp.int32, (n, n), 0)
    col = lax.broadcasted_iota(jnp.int32, (n, n), 1)
    return row, col


def cholesky_pair(gram):
    (packed,) = eliminate([gram])
    row, col = positions(gram.shape[0])
    pivots = jnp.sum(jnp.where(row == col, packed, 0.0), 1, keepdims=True)
    scale = 1.0 / jnp.sqrt(pivots)
    upper = jnp.where(col >= row, packed, 0.0) * scale
    inverse = jnp.where(col < row, packed, jnp.where(col == row, 1.0, 0.0)) * scale
    return upper, inverse


def split(x):
    high = x.astype(jnp.bfloat16)
    return high, (x - high.astype(jnp.float32)).astype(jnp.bfloat16)


def dot_split(left, right, dims=NN):
    small = dot(left[1], right[0], dims, None) + dot(left[0], right[1], dims, None)
    return small + dot(left[0], right[0], dims, None)


def four_sum(refs):
    one, two, three, four = (ref[...] for ref in refs)
    return (one + two) + (three + four)


def panel_kernel(place_ref, *refs):
    stacks, panel_ref, gram_ref = refs[:YS], refs[YS], refs[YS + 1]
    chunk = stacks[0].shape[1]
    y = place_ref[1] % YS
    for far, stack in enumerate(stacks):
        for z in range(ZS):
            at = (z * YS + (y ^ far)) * chunk
            panel_ref[pl.ds(pl.multiple_of(at, chunk), chunk), :] = stack[z]
    panel = panel_ref[...]
    gram_ref[...] = dot(panel, panel, TN)


def product_kernel(place_ref, panel_ref, gram_ref, trailing_ref, mine_ref, away_ref, halves_ref):
    rows, cols = trailing_ref.shape
    width = panel_ref.shape[1]
    tile = rows // PARTS
    leading = jnp.where(place_ref[0] == 0, panel_ref[:width, :], 0.0)
    total = jnp.zeros((width, cols), jnp.float32)
    for part in range(PARTS):
        span = slice(part * tile, (part + 1) * tile)
        total = total + dot(panel_ref[span, :], trailing_ref[span, :], TN)
    total = total.T
    for core in range(2):
        at = core * halves_ref.shape[0] // 2
        for block in (gram_ref[...], total, leading):
            part = block.shape[0] // 2
            halves_ref[at : at + part, :] = block[core * part : (core + 1) * part]
            at += part
    core = place_ref[0] % 2
    half = halves_ref.shape[0] // 2
    mine_ref[...] = halves_ref[pl.ds(pl.multiple_of(core * half, 8), half), :]
    away_ref[...] = halves_ref[pl.ds(pl.multiple_of((1 - core) * half, 8), half), :]


def first_kernel(place_ref, mine_ref, other_ref, panel_ref, upper_ref, upper_copy_ref, inverse_ref, ortho_ref, gram_ref):
    part = panel_ref.shape[1] // 2
    mine, other = mine_ref[:part, :], other_ref[:part, :]
    first = place_ref[0] % 2 == 0
    gram = jnp.concatenate([jnp.where(first, mine, other), jnp.where(first, other, mine)], 0)
    upper, inverse = cholesky_pair(gram)
    upper_ref[...] = upper
    upper_copy_ref[...] = upper
    inverse_ref[...] = inverse
    ortho = dot(panel_ref[...], inverse, NT)
    ortho_ref[...] = ortho
    gram_ref[...] = dot(ortho, ortho, TN)


def second_kernel(*refs):
    upper_one_ref, inverse_one_ref, leading_ref = refs[4:7]
    inverse_two_ref, band_ref, band_inverse_t_ref, square_ref = refs[7:]
    upper, inverse = cholesky_pair(four_sum(refs[:4]))
    row, col = positions(upper.shape[0])
    inverse_one = inverse_one_ref[...]
    inverse_two_ref[...] = inverse
    band_ref[...] = dot(upper, upper_one_ref[...])
    band_inverse_t_ref[...] = dot(inverse, inverse_one)
    top = dot(dot(leading_ref[...], inverse_one, NT), inverse, NT)
    square_ref[...] = top + jnp.where(row == col, 1.0, 0.0)


def third_kernel(square_ref, factor_ref, upper_inverse_ref, square_inverse_ref):
    square = square_ref[...]
    one, two = eliminate([square, square.T])
    row, col = positions(square.shape[0])
    unit = jnp.where(row == col, 1.0, 0.0)
    pivots = jnp.sum(jnp.where(row == col, two, 0.0), 1, keepdims=True)
    upper = jnp.where(col >= row, one, 0.0)
    lower_inverse = jnp.where(col < row, one, unit)
    upper_inverse = (jnp.where(col < row, two, unit) / pivots).T
    factor_ref[...] = dot(upper, lower_inverse, NT)
    upper_inverse_ref[...] = upper_inverse
    square_inverse_ref[...] = dot(upper_inverse, lower_inverse)


def block_call(body, outs, name, cost, args, **more):
    return pl.pallas_call(
        body,
        out_shape=[jax.ShapeDtypeStruct(shape, jnp.float32) for shape in outs],
        name=name,
        cost_estimate=pl.CostEstimate(flops=cost, bytes_accessed=1 << 20, transcendentals=0),
        compiler_params=pltpu.CompilerParams(vmem_limit_bytes=40 << 20),
        **more,
    )(*args)


def whole(count):
    return [pl.BlockSpec(memory_space=pltpu.VMEM)] * count


def scalars():
    return pl.BlockSpec(memory_space=pltpu.SMEM)


def unit_rows(start, count, width):
    place = start + lax.broadcasted_iota(jnp.int32, (count, width), 0)
    return jnp.where(place == lax.broadcasted_iota(jnp.int32, (count, width), 1), 1.0, 0.0)


def image_kernel(place_ref, *refs):
    products, edges = refs[:YS], refs[YS : 2 * YS]
    ortho_ref, inverse_two_ref, band_inverse_t_ref, base_ref, image_ref, weight_ref = refs[2 * YS :]
    cols, width = products[0].shape
    y = place_ref[1] % YS
    inverse_two = split(inverse_two_ref[...])
    band_inverse_t = band_inverse_t_ref[...]
    weight = jnp.zeros((width, width), jnp.float32)
    for far in range(YS):
        at = pl.multiple_of((y ^ far) * cols, cols)
        span = pl.ds(at, cols)
        start = place_ref[0] * (YS * cols) + at
        base = dot_split(split(ortho_ref[span, :]), inverse_two, NT) + unit_rows(start, cols, width)
        image = dot(products[far][...], band_inverse_t, NT) + edges[far][...]
        base_ref[span, :] = base
        image_ref[span, :] = image
        weight = weight + dot_split(split(base), split(image), TN)
    weight_ref[...] = weight


def left_kernel(place_ref, base_ref, panel_ref, product_ref, edge_ref, inverse_one_ref, inverse_two_ref, band_inverse_t_ref, square_inverse_ref, upper_inverse_ref, left_ref, reflectors_ref, left_cols_ref, image_cols_ref):
    rows, width = base_ref.shape
    cols = panel_ref.shape[0]
    square_inverse = square_inverse_ref[...]
    table = split(jnp.concatenate([square_inverse, upper_inverse_ref[...]], 1))
    both = dot_split(split(base_ref[...]), table)
    left_ref[...] = both[:, :width]
    place = place_ref[0] * rows + lax.broadcasted_iota(jnp.int32, (rows, width), 0)
    lane = lax.broadcasted_iota(jnp.int32, (rows, width), 1)
    reflectors_ref[...] = jnp.where(place < lane, 0.0, jnp.where(place == lane, 1.0, both[:, width:]))
    ortho = dot(panel_ref[...], inverse_one_ref[...], NT)
    base = dot_split(split(ortho), split(inverse_two_ref[...]), NT) + unit_rows(place_ref[1] * cols, cols, width)
    left_cols_ref[...] = dot_split(split(base), split(square_inverse))
    image_cols_ref[...] = dot(product_ref[...], band_inverse_t_ref[...], NT) + edge_ref[...]


def update_kernel(*refs):
    trailing_ref, left_ref, image_ref, left_cols_ref, image_cols_ref, updated_ref, high_ref, low_ref, weight_high_ref, weight_low_ref = refs[4:]

    @pl.when(pl.program_id(0) == 0)
    def _():
        weight_high_ref[...], weight_low_ref[...] = split(0.5 * four_sum(refs[:4]))
        weight = weight_high_ref[...], weight_low_ref[...]
        left = left_cols_ref[...]
        right = image_cols_ref[...] - dot_split(split(left), weight)
        high_ref[...], low_ref[...] = split(jnp.concatenate([right, left], 1))

    left = left_ref[...]
    pieces = split(left)
    right = image_ref[...] - dot_split(pieces, (weight_high_ref[...], weight_low_ref[...]))
    rights = split(right)
    pair = tuple(jnp.concatenate([one, two], 1) for one, two in zip(pieces, rights))
    updated_ref[...] = trailing_ref[...] - dot_split(pair, (high_ref[...], low_ref[...]), NT)


def update(weights, trailing, left, image, left_cols, image_cols, steps=4):
    rows, cols = trailing.shape
    width = left.shape[1]
    tile = rows // steps
    moving = lambda step: (step, 0)
    fixed = lambda step: (0, 0)
    range_spec = pl.BlockSpec((tile, width), moving)
    cols_spec = pl.BlockSpec((cols, width), fixed)
    square_spec = pl.BlockSpec((width, width), fixed)
    tile_spec = pl.BlockSpec((tile, cols), moving)
    return block_call(
        update_kernel,
        [(rows, cols)],
        "update",
        1 << 32,
        [*weights, trailing, left, image, left_cols, image_cols],
        grid=(steps,),
        in_specs=[square_spec] * 4 + [tile_spec] + [range_spec] * 2 + [cols_spec] * 2,
        out_specs=[tile_spec],
        scratch_shapes=[pltpu.VMEM((cols, 2 * width), jnp.bfloat16)] * 2
        + [pltpu.VMEM((width, width), jnp.bfloat16)] * 2,
    )[0]


def swap_row(x, mask):
    return lax.ppermute(x, "prow", [(r, r ^ mask) for r in range(ROWS)])


def swap_y(x, mask):
    return lax.ppermute(x, "pcol", [(c, c ^ mask) for c in range(ZS * YS)])


def turn_z(x):
    pairs = [(r, z, z ^ (r // 2 + 4 * (r % 2))) for r in range(ROWS) for z in range(ZS)]
    return lax.ppermute(x, ("prow", "pcol"), [(place_of(r, z, y), place_of(r, t, y)) for r, z, t in pairs for y in range(YS)])


def turn_row(x, back=False):
    pairs = [(r, z, z ^ (r // 2 + 4 * (r % 2))) for r in range(ROWS) for z in range(ZS)]
    moves = [(place_of(r, z, y), place_of(t, z, y)) for r, z, t in pairs for y in range(YS)]
    if back:
        moves = [(t, f) for f, t in moves]
    return lax.ppermute(x, ("prow", "pcol"), moves)


def place_of(r, z, y):
    return (r * ZS + z) * YS + y


def three_rows(x):
    return [x] + [swap_row(x, 2 * mask) for mask in (1, 2, 3)]


def along_y(x):
    return [x] + [swap_y(x, mask) for mask in range(1, YS)]


def hold(*arrays):
    return lax.optimization_barrier(arrays)


def on_device(trailing, panel):
    rows, cols = trailing.shape
    chunk, width = panel.shape
    square = (width, width)
    row_index = lax.axis_index("prow")
    col_index = lax.axis_index("pcol")
    core = row_index % 2
    y = col_index % YS
    place = jnp.stack([row_index, col_index]).astype(jnp.int32)

    lines = [[z * YS + at for z in range(ZS)] for at in range(YS)]
    copies = jnp.broadcast_to(panel[None], (ZS, chunk, width))
    source, copies = hold(trailing[:width], copies)
    stack = lax.all_to_all(copies, "pcol", 0, 0, axis_index_groups=lines)
    edge = source.T
    pair = lax.ppermute(edge, "prow", [(0, 1)])
    pair = jnp.where(row_index == 0, edge, pair)
    arrived = [
        lax.ppermute(pair, "prow", [(0, 2 * far), (1, 2 * far + 1)]) for far in (1, 2, 3)
    ]
    edge_cols = jnp.where(row_index < 2, pair, arrived[0] + arrived[1] + arrived[2])

    edge_turned = turn_z(edge_cols)
    half = (cols + 2 * width) // 2
    panel_rows, gram = block_call(
        panel_kernel,
        [(rows, width), square],
        "panel",
        1 << 32,
        [place] + along_y(stack),
        in_specs=[scalars()] + whole(YS),
        out_specs=whole(2),
    )
    mine, away = block_call(
        product_kernel,
        [(half, width)] * 2,
        "product",
        1 << 32,
        [place, panel_rows, gram, trailing],
        in_specs=[scalars()] + whole(3),
        out_specs=whole(2),
        scratch_shapes=[pltpu.VMEM((2 * half, width), jnp.float32)],
    )
    panel_rows, mine, away, edge_turned = hold(panel_rows, mine, away, edge_turned)

    edge_turned = turn_row(edge_turned)
    messages = three_rows(mine + swap_row(away, 1))
    panel_cols = lax.dynamic_slice_in_dim(panel_rows, y * cols, cols, 0)
    messages[1], edge_turned, panel_cols = hold(messages[1], edge_turned, panel_cols)
    edges = along_y(edge_turned)
    panel_cols = turn_row(panel_cols, back=True)

    mine = (messages[0] + messages[1]) + (messages[2] + messages[3])
    mine, other = hold(mine, swap_row(mine, 1))
    summed = jnp.where(
        core == 0, jnp.stack([mine, other], 0), jnp.stack([other, mine], 0)
    )
    product_cols = summed[:, width // 2 : (width + cols) // 2].reshape(cols, width)
    leading = summed[:, (width + cols) // 2 :].reshape(square)
    product_turned = turn_z(product_cols)
    upper_one, upper_copy, inverse_one, ortho_rows, gram = block_call(
        first_kernel,
        [square, square, square, (rows, width), square],
        "first",
        1 << 33,
        [place, mine, other, panel_rows],
        in_specs=[scalars()] + whole(3),
        out_specs=whole(5),
    )
    gram, product_turned, panel_cols, *edges = hold(gram, product_turned, panel_cols, *edges)

    gram, product_turned = hold(gram + swap_row(gram, 1), product_turned)
    product_turned = turn_row(product_turned)
    panel_cols = turn_z(panel_cols)
    grams = three_rows(gram)
    *grams, product_turned, panel_cols = hold(*grams, product_turned, panel_cols)

    turned = along_y(product_turned)
    inverse_two, band_block, band_inverse_t, top = block_call(
        second_kernel, [square] * 4, "second", 1 << 33, grams + [upper_copy, inverse_one, leading],
        in_specs=whole(7), out_specs=whole(4),
    )
    factor, upper_inverse, square_inverse = block_call(
        third_kernel, [square] * 3, "third", 1 << 33, [top], in_specs=whole(1), out_specs=whole(3)
    )
    square_inverse, *turned = hold(square_inverse, *turned)
    base, image, weight = block_call(
        image_kernel,
        [(rows, width)] * 2 + [square],
        "image",
        1 << 31,
        [place] + turned + edges + [ortho_rows, inverse_two, band_inverse_t],
        in_specs=[scalars()] + whole(2 * YS + 3),
        out_specs=whole(3),
    )

    weight = weight + swap_row(weight, 1)
    weight, base = hold(weight, base)
    weights = three_rows(weight)
    left, reflectors, left_cols, image_cols = block_call(
        left_kernel,
        [(rows, width)] * 2 + [(cols, width)] * 2,
        "left",
        1 << 31,
        [place, base, panel_cols, product_cols, edge_cols, inverse_one, inverse_two, band_inverse_t, square_inverse, upper_inverse],
        in_specs=[scalars()] + whole(9),
        out_specs=whole(4),
    )
    updated = update(weights, trailing, left, image, left_cols, image_cols)
    return (updated, reflectors, factor, band_block, upper_one)


def solution(mesh):
    placed = (P("prow", "pcol"), P(("prow", "pcol"), None))
    return jax.shard_map(
        on_device,
        mesh=mesh,
        in_specs=placed,
        out_specs=(P("prow", "pcol"), P("prow", None), P(), P(), P()),
        check_vma=False,
    )
```

```python
import functools

import jax
import jax.numpy as jnp
from jax import lax
from jax.experimental import pallas as pl
from jax.experimental.pallas import tpu as pltpu
from jax.sharding import PartitionSpec as P

HIGHEST = lax.Precision.HIGHEST
ROWS, ZS, YS = 8, 8, 4
PARTS = 4
NN = (((1,), (0,)), ((), ()))
NT = (((1,), (1,)), ((), ()))
TN = (((0,), (0,)), ((), ()))


def dot(left, right, dims=NN, precision=HIGHEST):
    return lax.dot_general(
        left, right, dims, precision=precision, preferred_element_type=jnp.float32
    )


def eliminate(mats):
    n = mats[0].shape[0]
    lane = lax.broadcasted_iota(jnp.int32, (8, n), 1)
    sub = lax.broadcasted_iota(jnp.int32, (8, n), 0)
    across = lambda x, k: jnp.broadcast_to(x[:, k : k + 1], (8, n))
    down = lambda x, s: jnp.broadcast_to(x[s : s + 1], (8, n))
    tiles = [[m[8 * t : 8 * t + 8] for t in range(n // 8)] for m in mats]
    for t in range(n // 8):
        base = 8 * t
        block = (lane >= base) & (lane < base + 8)
        for m in tiles:
            cols = [across(m[t], base + s) for s in range(8)]
            work = m[t]
            invs, rows, heads = [], [], []
            for s in range(8):
                here = lane == base + s
                below = sub > s
                inv = pl.reciprocal(down(cols[s], s), approx=True)
                row = jnp.where(here, 1.0, down(work, s))
                low = jnp.where(below, cols[s], 0.0)
                work = jnp.where(here & below, 0.0, work) - (low * row) * inv
                head = [down(cols[q], s) for q in range(s + 1, 8)]
                for q in range(s + 1, 8):
                    cols[q] = cols[q] - (low * head[q - s - 1]) * inv
                invs.append(inv)
                rows.append(jnp.where(block & (lane > base + s), 0.0, row))
                heads.append(head)
            m[t] = work
            for j in range(t + 1, n // 8):
                cols = [across(m[j], base + s) for s in range(8)]
                new = jnp.where(block, 0.0, m[j])
                for s in range(8):
                    mult = cols[s] * invs[s]
                    new = new - mult * rows[s]
                    for q in range(s + 1, 8):
                        cols[q] = cols[q] - mult * heads[s][q - s - 1]
                m[j] = new
    return [jnp.concatenate(m, 0) for m in tiles]


def positions(n):
    row = lax.broadcasted_iota(jnp.int32, (n, n), 0)
    col = lax.broadcasted_iota(jnp.int32, (n, n), 1)
    return row, col


def cholesky_pair(gram):
    (packed,) = eliminate([gram])
    row, col = positions(gram.shape[0])
    pivots = jnp.sum(jnp.where(row == col, packed, 0.0), 1, keepdims=True)
    scale = 1.0 / jnp.sqrt(pivots)
    upper = jnp.where(col >= row, packed, 0.0) * scale
    inverse = jnp.where(col < row, packed, jnp.where(col == row, 1.0, 0.0)) * scale
    return upper, inverse


def split(x):
    high = x.astype(jnp.bfloat16)
    return high, (x - high.astype(jnp.float32)).astype(jnp.bfloat16)


def dot_split(left, right, dims=NN):
    small = dot(left[1], right[0], dims, None) + dot(left[0], right[1], dims, None)
    return small + dot(left[0], right[0], dims, None)


def four_sum(refs):
    one, two, three, four = (ref[...] for ref in refs)
    return (one + two) + (three + four)


def panel_kernel(place_ref, *refs):
    stacks, panel_ref, gram_ref = refs[:YS], refs[YS], refs[YS + 1]
    chunk = stacks[0].shape[1]
    y = place_ref[1] % YS
    for far, stack in enumerate(stacks):
        for z in range(ZS):
            at = (z * YS + (y ^ far)) * chunk
            panel_ref[pl.ds(pl.multiple_of(at, chunk), chunk), :] = stack[z]
    panel = panel_ref[...]
    gram_ref[...] = dot(panel, panel, TN)


def product_kernel(place_ref, panel_ref, gram_ref, trailing_ref, mine_ref, away_ref, halves_ref):
    rows, cols = trailing_ref.shape
    width = panel_ref.shape[1]
    tile = rows // PARTS
    leading = jnp.where(place_ref[0] == 0, panel_ref[:width, :], 0.0)
    total = jnp.zeros((width, cols), jnp.float32)
    for part in range(PARTS):
        span = slice(part * tile, (part + 1) * tile)
        total = total + dot(panel_ref[span, :], trailing_ref[span, :], TN)
    total = total.T
    for core in range(2):
        at = core * halves_ref.shape[0] // 2
        for block in (gram_ref[...], total, leading):
            part = block.shape[0] // 2
            halves_ref[at : at + part, :] = block[core * part : (core + 1) * part]
            at += part
    core = place_ref[0] % 2
    half = halves_ref.shape[0] // 2
    mine_ref[...] = halves_ref[pl.ds(pl.multiple_of(core * half, 8), half), :]
    away_ref[...] = halves_ref[pl.ds(pl.multiple_of((1 - core) * half, 8), half), :]


def first_kernel(place_ref, mine_ref, other_ref, panel_ref, upper_ref, upper_copy_ref, inverse_ref, ortho_ref, gram_ref):
    part = panel_ref.shape[1] // 2
    mine, other = mine_ref[:part, :], other_ref[:part, :]
    first = place_ref[0] % 2 == 0
    gram = jnp.concatenate([jnp.where(first, mine, other), jnp.where(first, other, mine)], 0)
    upper, inverse = cholesky_pair(gram)
    upper_ref[...] = upper
    upper_copy_ref[...] = upper
    inverse_ref[...] = inverse
    ortho = dot(panel_ref[...], inverse, NT)
    ortho_ref[...] = ortho
    gram_ref[...] = dot(ortho, ortho, TN)


def second_kernel(*refs):
    upper_one_ref, inverse_one_ref, leading_ref = refs[4:7]
    inverse_two_ref, band_ref, band_inverse_t_ref, square_ref = refs[7:]
    upper, inverse = cholesky_pair(four_sum(refs[:4]))
    row, col = positions(upper.shape[0])
    inverse_one = inverse_one_ref[...]
    inverse_two_ref[...] = inverse
    band_ref[...] = dot(upper, upper_one_ref[...])
    band_inverse_t_ref[...] = dot(inverse, inverse_one)
    top = dot(dot(leading_ref[...], inverse_one, NT), inverse, NT)
    square_ref[...] = top + jnp.where(row == col, 1.0, 0.0)


def third_kernel(square_ref, factor_ref, upper_inverse_ref, square_inverse_ref):
    square = square_ref[...]
    one, two = eliminate([square, square.T])
    row, col = positions(square.shape[0])
    unit = jnp.where(row == col, 1.0, 0.0)
    pivots = jnp.sum(jnp.where(row == col, two, 0.0), 1, keepdims=True)
    upper = jnp.where(col >= row, one, 0.0)
    lower_inverse = jnp.where(col < row, one, unit)
    upper_inverse = (jnp.where(col < row, two, unit) / pivots).T
    factor_ref[...] = dot(upper, lower_inverse, NT)
    upper_inverse_ref[...] = upper_inverse
    square_inverse_ref[...] = dot(upper_inverse, lower_inverse)


def block_call(body, outs, name, cost, args, **more):
    return pl.pallas_call(
        body,
        out_shape=[jax.ShapeDtypeStruct(shape, jnp.float32) for shape in outs],
        name=name,
        cost_estimate=pl.CostEstimate(flops=cost, bytes_accessed=1 << 20, transcendentals=0),
        compiler_params=pltpu.CompilerParams(vmem_limit_bytes=40 << 20),
        **more,
    )(*args)


def whole(count):
    return [pl.BlockSpec(memory_space=pltpu.VMEM)] * count


def scalars():
    return pl.BlockSpec(memory_space=pltpu.SMEM)


def unit_rows(start, count, width):
    place = start + lax.broadcasted_iota(jnp.int32, (count, width), 0)
    return jnp.where(place == lax.broadcasted_iota(jnp.int32, (count, width), 1), 1.0, 0.0)


def image_kernel(place_ref, *refs):
    products, edges = refs[:YS], refs[YS : 2 * YS]
    ortho_ref, inverse_two_ref, band_inverse_t_ref, base_ref, image_ref, weight_ref = refs[2 * YS :]
    cols, width = products[0].shape
    y = place_ref[1] % YS
    inverse_two = split(inverse_two_ref[...])
    band_inverse_t = band_inverse_t_ref[...]
    weight = jnp.zeros((width, width), jnp.float32)
    for far in range(YS):
        at = pl.multiple_of((y ^ far) * cols, cols)
        span = pl.ds(at, cols)
        start = place_ref[0] * (YS * cols) + at
        base = dot_split(split(ortho_ref[span, :]), inverse_two, NT) + unit_rows(start, cols, width)
        image = dot(products[far][...], band_inverse_t, NT) + edges[far][...]
        base_ref[span, :] = base
        image_ref[span, :] = image
        weight = weight + dot_split(split(base), split(image), TN)
    weight_ref[...] = weight


def left_kernel(place_ref, base_ref, panel_ref, product_ref, edge_ref, inverse_one_ref, inverse_two_ref, band_inverse_t_ref, square_inverse_ref, upper_inverse_ref, left_ref, reflectors_ref, left_cols_ref, image_cols_ref):
    rows, width = base_ref.shape
    cols = panel_ref.shape[0]
    square_inverse = square_inverse_ref[...]
    table = split(jnp.concatenate([square_inverse, upper_inverse_ref[...]], 1))
    both = dot_split(split(base_ref[...]), table)
    left_ref[...] = both[:, :width]
    place = place_ref[0] * rows + lax.broadcasted_iota(jnp.int32, (rows, width), 0)
    lane = lax.broadcasted_iota(jnp.int32, (rows, width), 1)
    reflectors_ref[...] = jnp.where(place < lane, 0.0, jnp.where(place == lane, 1.0, both[:, width:]))
    ortho = dot(panel_ref[...], inverse_one_ref[...], NT)
    base = dot_split(split(ortho), split(inverse_two_ref[...]), NT) + unit_rows(place_ref[1] * cols, cols, width)
    left_cols_ref[...] = dot_split(split(base), split(square_inverse))
    image_cols_ref[...] = dot(product_ref[...], band_inverse_t_ref[...], NT) + edge_ref[...]


def update_kernel(*refs):
    trailing_ref, left_ref, image_ref, left_cols_ref, image_cols_ref, updated_ref, high_ref, low_ref, weight_high_ref, weight_low_ref = refs[4:]

    @pl.when(pl.program_id(0) == 0)
    def _():
        weight_high_ref[...], weight_low_ref[...] = split(0.5 * four_sum(refs[:4]))
        weight = weight_high_ref[...], weight_low_ref[...]
        left = left_cols_ref[...]
        right = image_cols_ref[...] - dot_split(split(left), weight)
        high_ref[...], low_ref[...] = split(jnp.concatenate([right, left], 1))

    left = left_ref[...]
    pieces = split(left)
    right = image_ref[...] - dot_split(pieces, (weight_high_ref[...], weight_low_ref[...]))
    rights = split(right)
    pair = tuple(jnp.concatenate([one, two], 1) for one, two in zip(pieces, rights))
    updated_ref[...] = trailing_ref[...] - dot_split(pair, (high_ref[...], low_ref[...]), NT)


def update(weights, trailing, left, image, left_cols, image_cols, steps=2):
    rows, cols = trailing.shape
    width = left.shape[1]
    tile = rows // steps
    moving = lambda step: (step, 0)
    fixed = lambda step: (0, 0)
    range_spec = pl.BlockSpec((tile, width), moving)
    cols_spec = pl.BlockSpec((cols, width), fixed)
    square_spec = pl.BlockSpec((width, width), fixed)
    tile_spec = pl.BlockSpec((tile, cols), moving)
    return block_call(
        update_kernel,
        [(rows, cols)],
        "update",
        1 << 32,
        [*weights, trailing, left, image, left_cols, image_cols],
        grid=(steps,),
        in_specs=[square_spec] * 4 + [tile_spec] + [range_spec] * 2 + [cols_spec] * 2,
        out_specs=[tile_spec],
        scratch_shapes=[pltpu.VMEM((cols, 2 * width), jnp.bfloat16)] * 2
        + [pltpu.VMEM((width, width), jnp.bfloat16)] * 2,
    )[0]


def swap_row(x, mask):
    return lax.ppermute(x, "prow", [(r, r ^ mask) for r in range(ROWS)])


def swap_y(x, mask):
    return lax.ppermute(x, "pcol", [(c, c ^ mask) for c in range(ZS * YS)])


def turn_z(x):
    pairs = [(r, z, z ^ (r // 2 + 4 * (r % 2))) for r in range(ROWS) for z in range(ZS)]
    return lax.ppermute(x, ("prow", "pcol"), [(place_of(r, z, y), place_of(r, t, y)) for r, z, t in pairs for y in range(YS)])


def turn_row(x, back=False):
    pairs = [(r, z, z ^ (r // 2 + 4 * (r % 2))) for r in range(ROWS) for z in range(ZS)]
    moves = [(place_of(r, z, y), place_of(t, z, y)) for r, z, t in pairs for y in range(YS)]
    if back:
        moves = [(t, f) for f, t in moves]
    return lax.ppermute(x, ("prow", "pcol"), moves)


def place_of(r, z, y):
    return (r * ZS + z) * YS + y


def three_rows(x):
    return [x] + [swap_row(x, 2 * mask) for mask in (1, 2, 3)]


def along_y(x):
    return [x] + [swap_y(x, mask) for mask in range(1, YS)]


def hold(*arrays):
    return lax.optimization_barrier(arrays)


def on_device(trailing, panel):
    rows, cols = trailing.shape
    chunk, width = panel.shape
    square = (width, width)
    row_index = lax.axis_index("prow")
    col_index = lax.axis_index("pcol")
    core = row_index % 2
    y = col_index % YS
    place = jnp.stack([row_index, col_index]).astype(jnp.int32)

    lines = [[z * YS + at for z in range(ZS)] for at in range(YS)]
    copies = jnp.broadcast_to(panel[None], (ZS, chunk, width))
    source, copies = hold(trailing[:width], copies)
    stack = lax.all_to_all(copies, "pcol", 0, 0, axis_index_groups=lines)
    edge = source.T
    pair = lax.ppermute(edge, "prow", [(0, 1)])
    pair = jnp.where(row_index == 0, edge, pair)
    arrived = [
        lax.ppermute(pair, "prow", [(0, 2 * far), (1, 2 * far + 1)]) for far in (1, 2, 3)
    ]
    edge_cols = jnp.where(row_index < 2, pair, arrived[0] + arrived[1] + arrived[2])

    edge_turned = turn_z(edge_cols)
    half = (cols + 2 * width) // 2
    panel_rows, gram = block_call(
        panel_kernel,
        [(rows, width), square],
        "panel",
        1 << 32,
        [place] + along_y(stack),
        in_specs=[scalars()] + whole(YS),
        out_specs=whole(2),
    )
    mine, away = block_call(
        product_kernel,
        [(half, width)] * 2,
        "product",
        1 << 32,
        [place, panel_rows, gram, trailing],
        in_specs=[scalars()] + whole(3),
        out_specs=whole(2),
        scratch_shapes=[pltpu.VMEM((2 * half, width), jnp.float32)],
    )
    panel_rows, mine, away, edge_turned = hold(panel_rows, mine, away, edge_turned)

    edge_turned = turn_row(edge_turned)
    messages = three_rows(mine + swap_row(away, 1))
    panel_cols = lax.dynamic_slice_in_dim(panel_rows, y * cols, cols, 0)
    messages[1], edge_turned, panel_cols = hold(messages[1], edge_turned, panel_cols)
    edges = along_y(edge_turned)
    panel_cols = turn_row(panel_cols, back=True)

    mine = (messages[0] + messages[1]) + (messages[2] + messages[3])
    mine, other, edges[1] = hold(mine, swap_row(mine, 1), edges[1])
    summed = jnp.where(
        core == 0, jnp.stack([mine, other], 0), jnp.stack([other, mine], 0)
    )
    product_cols = summed[:, width // 2 : (width + cols) // 2].reshape(cols, width)
    leading = summed[:, (width + cols) // 2 :].reshape(square)
    product_turned = turn_z(product_cols)
    upper_one, upper_copy, inverse_one, ortho_rows, gram = block_call(
        first_kernel,
        [square, square, square, (rows, width), square],
        "first",
        1 << 33,
        [place, mine, other, panel_rows],
        in_specs=[scalars()] + whole(3),
        out_specs=whole(5),
    )
    gram, product_turned, panel_cols, *edges = hold(gram, product_turned, panel_cols, *edges)

    gram, product_turned = hold(gram + swap_row(gram, 1), product_turned)
    product_turned = turn_row(product_turned)
    panel_cols = turn_z(panel_cols)
    grams = three_rows(gram)
    *grams, product_turned, panel_cols = hold(*grams, product_turned, panel_cols)

    turned = along_y(product_turned)
    inverse_two, band_block, band_inverse_t, top = block_call(
        second_kernel, [square] * 4, "second", 1 << 33, grams + [upper_copy, inverse_one, leading],
        in_specs=whole(7), out_specs=whole(4),
    )
    factor, upper_inverse, square_inverse = block_call(
        third_kernel, [square] * 3, "third", 1 << 33, [top], in_specs=whole(1), out_specs=whole(3)
    )
    square_inverse, *turned = hold(square_inverse, *turned)
    base, image, weight = block_call(
        image_kernel,
        [(rows, width)] * 2 + [square],
        "image",
        1 << 31,
        [place] + turned + edges + [ortho_rows, inverse_two, band_inverse_t],
        in_specs=[scalars()] + whole(2 * YS + 3),
        out_specs=whole(3),
    )

    weight = weight + swap_row(weight, 1)
    weight, base = hold(weight, base)
    weights = three_rows(weight)
    left, reflectors, left_cols, image_cols = block_call(
        left_kernel,
        [(rows, width)] * 2 + [(cols, width)] * 2,
        "left",
        1 << 31,
        [place, base, panel_cols, product_cols, edge_cols, inverse_one, inverse_two, band_inverse_t, square_inverse, upper_inverse],
        in_specs=[scalars()] + whole(9),
        out_specs=whole(4),
    )
    updated = update(weights, trailing, left, image, left_cols, image_cols)
    return (updated, reflectors, factor, band_block, upper_one)


def solution(mesh):
    placed = (P("prow", "pcol"), P(("prow", "pcol"), None))
    return jax.shard_map(
        on_device,
        mesh=mesh,
        in_specs=placed,
        out_specs=(P("prow", "pcol"), P("prow", None), P(), P(), P()),
        check_vma=False,
    )
```
